128 devices in a mesh: slab: 8 (over y_lo, x), sector: 16 (over y_hi, z, core).
Axes of the slice: x: 4, y: 4 (y_hi: 2, y_lo: 2; y = y_hi * 2 + y_lo), z: 4, core: 2. Of those that a mesh axis runs over, the one named last changes fastest.
Arguments:
- velocity: float32 [3, 128, 1024, 768], P(None, 'slab', 'sector'), may hold values from -4 to 4
- pressure: float32 [128, 1024, 768], P('slab', 'sector'), may hold values from -4 to 4
- disk_cell: int32 [8, 8192], P('slab', 'sector'), may hold values from 0 to 786431, as said below
- disk_count: int32 [8, 16], P('slab', 'sector'), may hold values from 256 to 512, as said below
- disk_owner: int32 [8, 8192, 1], P('slab', 'sector'), may hold values from 0 to 15; in each aligned block of 512 rows (0 to 511, 512 to 1023, ..., all dimensions but the last counted through in order) at most 48 rows name the same one
- disk_section: int32 [8, 8192], P('slab', 'sector'), may hold values from 0 to 63
- polar: float32 [2, 1024, 256], P(None, 'sector'), may hold values from -1 to 1.5
- geometry: float32 [2, 1024], P(None, 'sector'), may hold values from 0.02 to 0.2
Outputs:
- corrected: float32 [3, 128, 1024, 768], P(None, 'slab', 'sector')
- settled: float32 [128, 1024, 768], P('slab', 'sector')
- section_loads: float32 [2, 1024], P(None, 'sector')
The draws below stay inside these ranges and needn't reach their ends.
Inputs may be any that keep to these rules, and one draw needn't show every extreme that they name: `disk_cell`: within one device's slots the cells are distinct. `disk_count`: some device uses all 512 slots. `disk_owner`: among the slots of one device at most 48 name the same owner, and exactly 48 do on some device.
All inputs are finite; a program needn't handle non-finite values.
Results may differ from the reference program's by a relative error of at most 0.0003.
Values sent between devices are 32-bit elements; how exact they have to be, the bound alone decides.
A program may use at most 192 MiB of HBM per device.

```python
import math
import jax
import jax.numpy as jnp
import numpy as np
from jax import lax

CX = 16
CY = 64
CZ = 768
SLOTS = 512
SEC_DEV = 64
ANG = 256
CAP = 48
SECTIONS = 1024
NX = 128
NY = 1024
N_SLAB = 8
N_SECTOR = 16


def draw_disk_cell(key, part):
    key = jax.random.fold_in(key, 11)
    stride = CX * CY * CZ // SLOTS
    starts = jnp.arange(N_SECTOR * SLOTS, dtype=jnp.int32) % SLOTS * stride
    offsets = jax.random.randint(key, (N_SLAB, N_SECTOR * SLOTS), 0, stride, dtype=jnp.int32)
    cell_ids = starts[None, :] + offsets
    cell_ids = cell_ids.at[0, 0].set(0)
    cell_ids = cell_ids.at[0, SLOTS - 1].set(CX * CY * CZ - 1)
    return cell_ids.astype(jnp.int32)


def draw_disk_count(key, part):
    key = jax.random.fold_in(key, 12)
    counts = jax.random.randint(key, (N_SLAB * N_SECTOR,), SLOTS // 2, SLOTS + 1, dtype=jnp.int32)
    chosen = jax.random.randint(jax.random.fold_in(key, 1), (), 0, N_SLAB * N_SECTOR, dtype=jnp.int32)
    counts = counts.at[chosen].set(SLOTS)
    return counts.reshape(N_SLAB, N_SECTOR).astype(jnp.int32)


def place_ends(array, rng, smallest, high):
    extent = array.shape
    index_at = [jax.random.randint(jax.random.fold_in(rng, axis), (), 0, extent[axis]) for axis in range(len(extent))]
    array = array.at[tuple(index_at)].set(smallest)
    longest = extent.index(max(extent))
    index_at[longest] = (index_at[longest] + 1) % extent[longest]
    return array.at[tuple(index_at)].set(high)


def shard_levels(own_key, extent, split, smallest, top_value):
    def one(axis_at, shards_of):
        heights = jax.random.uniform(jax.random.fold_in(jax.random.fold_in(own_key, 6), axis_at), (shards_of,), jnp.float32, smallest / len(split), top_value / len(split))
        return jnp.repeat(jnp.exp(heights), extent[axis_at] // shards_of).reshape((-1,) + (1,) * (len(extent) - axis_at - 1))

    gain = one(*split[0])
    for cut in split[1:]:
        gain = gain * one(*cut)
    return gain


def deal_out(own_key, own, number, rows, number_of, top, bound, slope):
    order = jax.random.permutation(own_key, number_of)
    heavy_load, usual = load_shares(number_of, rows * top, bound, slope, True), load_shares(number_of, rows * top, bound, slope, False)
    places = jnp.arange(number_of)

    def named(tallies, offset_by):
        used = int((tallies > 0).sum())
        fixed = max(1, used // 4)
        moved = fixed + (places - fixed + offset_by * (used - fixed)) % max(1, number_of - fixed)
        return jnp.zeros((number_of,), jnp.int32).at[order[jnp.where(places < fixed, places, moved)]].set(jnp.asarray(tallies, jnp.int32))

    tallies = jnp.where(number % 4 == 0, named(heavy_load, number // 4), named(usual, number - number // 4 - 1))
    mixed = jax.random.permutation(jax.random.fold_in(own, 3), number_of)
    source_of, receiver = mixed[0:number_of // 2 * 2:2], mixed[1:number_of // 2 * 2:2]
    room = jnp.minimum(tallies[source_of] - 1, bound - tallies[receiver]) // 2
    room = jnp.where((source_of == order[0]) | (receiver == order[0]) | (tallies[receiver] == 0), 0, jnp.maximum(room, 0))
    moved = jax.random.randint(jax.random.fold_in(own, 4), (number_of // 2,), 0, 1 << 20) % (room + 1)
    tallies = tallies.at[source_of].add(-moved).at[receiver].add(moved)
    labels = jnp.searchsorted(jnp.cumsum(tallies), jnp.arange(rows * top), side="right").astype(jnp.int32)
    table = labels.reshape(top, rows).T
    table = table[jax.random.permutation(jax.random.fold_in(own, 1), rows)]
    offset_by = jax.random.randint(jax.random.fold_in(own, 2), (rows, 1), 0, top)
    return jnp.take_along_axis(table, (jnp.arange(top)[None, :] + offset_by) % top, axis=1)


def load_shares(amount, total, limit, lean, full):
    loads = [(1 << 20) // math.isqrt(rank ** lean) + 1 for rank in range(1, amount + 1)]
    largest = limit if full else min(limit, max(-(-total // amount), total * loads[0] // sum(loads)))
    least = 1 if total - largest >= amount - 1 else 0
    given, surplus = [largest] + [least] * (amount - 1), total - largest - least * (amount - 1)
    while surplus > 0:
        free = [i for i in range(1, amount) if given[i] < largest] or [i for i in range(1, amount) if given[i] < limit]
        mass, budget = sum([loads[i] for i in free]), surplus
        for i in free:
            more = min(limit - given[i], max(1, budget * loads[i] // mass), surplus)
            given[i] = given[i] + more
            surplus = surplus - more
    return np.array(given)


def noise(key, extent, spread, bound, pieces=(), kind=jnp.bfloat16):
    result = jax.random.normal(key, extent, jnp.float32) * spread
    if len(pieces) > 0:
        result = shard_levels(key, extent, pieces, -0.22, 0.18) * result
    return jnp.clip(result, min=-bound, max=bound).astype(kind)


def setup_inputs(seed: int = 0) -> dict:
    streams_of = jax.random.split(jax.random.key(seed), 9)
    velocity = noise(streams_of[0], (3, NX, NY, CZ), 0.25, 4.0, ((1, 8), (2, 16)), jnp.float32)
    pressure = noise(streams_of[1], (NX, NY, CZ), 0.25, 4.0, ((0, 8), (1, 16)), jnp.float32)
    disk_cell = draw_disk_cell(jax.random.fold_in(streams_of[8], 71), 0)
    disk_count = draw_disk_count(jax.random.fold_in(streams_of[8], 71), 0)
    disk_owner_keys = jax.random.split(jax.random.fold_in(streams_of[4], 1), N_SLAB * (N_SECTOR * SLOTS) // SLOTS)
    disk_owner_turns = jax.random.permutation(jax.random.fold_in(streams_of[4], 3), N_SLAB * (N_SECTOR * SLOTS) // SLOTS)
    disk_owner = jax.vmap(lambda own, number: deal_out(jax.random.fold_in(streams_of[4], 2), own, number, SLOTS, N_SECTOR, 1, CAP, 2))(disk_owner_keys, disk_owner_turns).reshape((N_SLAB, N_SECTOR * SLOTS, 1))
    disk_section = place_ends(jax.random.randint(streams_of[5], (N_SLAB, N_SECTOR * SLOTS), 0, SEC_DEV), jax.random.fold_in(streams_of[5], 1), 0, SEC_DEV - 1).astype(jnp.int32)
    polar = jnp.clip(-1.0 + 2.5 * jax.random.uniform(streams_of[6], (2, SECTIONS, ANG), jnp.float32) ** shard_levels(streams_of[6], (2, SECTIONS, ANG), ((1, 16),), -0.2, 0.2), -1.0, 1.5)
    geometry = jnp.clip(jnp.exp(math.log(0.2) - 2.3025851 * jax.random.uniform(streams_of[7], (2, SECTIONS), jnp.float32) ** shard_levels(streams_of[7], (2, SECTIONS), ((1, 16),), -0.2, 0.2)), 0.02, 0.2)
    return dict(velocity=velocity, pressure=pressure, disk_cell=disk_cell, disk_count=disk_count, disk_owner=disk_owner, disk_section=disk_section, polar=polar, geometry=geometry)


viscous = 0.1
pressure_step = 0.5
inflow = 1.0
rotation = 10.0
forcing = 0.2
alpha_span = 2.0


def shifted(scalar, dim_pos, offset, periodic):
    if periodic:
        return jnp.roll(scalar, -offset, dim_pos)
    length_here = scalar.shape[dim_pos]
    widths = [(0, 0)] * scalar.ndim
    widths[dim_pos] = (1, 1)
    padded = jnp.pad(scalar, widths)
    return lax.slice_in_dim(padded, 1 + offset, 1 + offset + length_here, axis=dim_pos)


def neighbour_sum(scalar):
    first_dim = scalar.ndim - 3
    summed = shifted(scalar, first_dim, 1, False) + shifted(scalar, first_dim, -1, False)
    summed = summed + shifted(scalar, first_dim + 1, 1, True) + shifted(scalar, first_dim + 1, -1, True)
    summed = summed + shifted(scalar, first_dim + 2, 1, False) + shifted(scalar, first_dim + 2, -1, False)
    return summed


def central(scalar, dim_pos, periodic):
    return 0.5 * (shifted(scalar, dim_pos, 1, periodic) - shifted(scalar, dim_pos, -1, periodic))


def gradient(scalar):
    return jnp.stack([central(scalar, 0, False), central(scalar, 1, True), central(scalar, 2, False)])


def divergence(flow):
    return central(flow[0], 0, False) + central(flow[1], 1, True) + central(flow[2], 2, False)


def blade_forces(axial_part, turning, radius, chord_len, twist_ang, lift_rows, drag_rows, bin_total):
    axial_speed = inflow + axial_part
    tangent_speed = rotation * radius + turning
    inflow_angle = jnp.arctan2(axial_speed, tangent_speed)
    position = (inflow_angle - twist_ang + alpha_span) * ((bin_total - 1) / (2.0 * alpha_span))
    bin_ids = jnp.arange(bin_total, dtype=jnp.float32)
    weights = jnp.maximum(0.0, 1.0 - jnp.abs(position[..., None] - bin_ids))
    lift_coef = jnp.sum(lift_rows * weights, -1)
    drag_coef = jnp.sum(drag_rows * weights, -1)
    dynamic = 0.5 * (axial_speed * axial_speed + tangent_speed * tangent_speed) * chord_len
    cosine = jnp.cos(inflow_angle)
    sine = jnp.sin(inflow_angle)
    thrust = dynamic * (lift_coef * cosine - drag_coef * sine)
    swirl_force = dynamic * (lift_coef * sine + drag_coef * cosine)
    return thrust, swirl_force


def reference(velocity, pressure, disk_cell, disk_count, disk_owner, disk_section, polar, geometry):
    predicted = velocity + viscous * (neighbour_sum(velocity) - 6.0 * velocity) - pressure_step * gradient(pressure)
    slot_ids = jnp.arange(N_SECTOR * SLOTS, dtype=jnp.int32)
    column = slot_ids // SLOTS
    usable = (slot_ids % SLOTS)[None, :] < disk_count[:, column]
    local_x = disk_cell // (CY * CZ)
    local_y = (disk_cell // CZ) % CY
    local_z = disk_cell % CZ
    global_x = (jnp.arange(N_SLAB, dtype=jnp.int32) * CX)[:, None] + local_x
    global_y = (column * CY)[None, :] + local_y
    global_x = global_x.reshape(-1)
    global_y = global_y.reshape(-1)
    local_z = local_z.reshape(-1)
    axial_part = predicted[0, global_x, global_y, local_z]
    turning = predicted[1, global_x, global_y, local_z]
    radius = 0.25 + 0.75 * (local_z.astype(jnp.float32) + 0.5) / CZ
    section = (disk_owner[..., 0] * SEC_DEV + disk_section).reshape(-1).astype(jnp.int32)
    active = usable.reshape(-1).astype(jnp.float32)
    thrust, swirl_force = blade_forces(axial_part, turning, radius, geometry[0][section], geometry[1][section], polar[0][section], polar[1][section], ANG)
    thrust = thrust * active
    swirl_force = swirl_force * active
    pushed = predicted.at[0, global_x, global_y, local_z].add(forcing * thrust)
    pushed = pushed.at[1, global_x, global_y, local_z].add(forcing * swirl_force)
    section_loads = jnp.stack([jax.ops.segment_sum(thrust, section, SECTIONS), jax.ops.segment_sum(swirl_force * radius, section, SECTIONS)])
    source = divergence(pushed)
    press_now = pressure
    for sweep_index in range(2):
        press_now = (neighbour_sum(press_now) - source) / 6.0
    corrected = pushed - gradient(press_now)
    return corrected, press_now, section_loads
```

```python
import functools

import jax
import jax.numpy as jnp
from jax import lax
from jax.experimental import pallas as pl
from jax.experimental.pallas import tpu as pltpu
from jax.sharding import PartitionSpec as P

MESH = pl.DeviceIdType.MESH
F32 = jnp.float32
I32 = jnp.int32
BF16 = jnp.bfloat16
L = 128
PAD = 8


def z_pair(tiles, lane):
    up = [pltpu.roll(t, L - 1, 1) for t in tiles]
    down = [pltpu.roll(t, 1, 1) for t in tiles]
    last = len(tiles) - 1
    zero = jnp.zeros_like(tiles[0])
    after = [jnp.where(lane == L - 1, up[j + 1] if j < last else zero, up[j]) for j in range(last + 1)]
    before = [jnp.where(lane == 0, down[j - 1] if j > 0 else zero, down[j]) for j in range(last + 1)]
    return after, before


def kernel(
    n_slab,
    n_sector,
    vel,
    pre,
    cell_h,
    owner_h,
    section_h,
    polar,
    geometry_h,
    count_s,
    out,
    out_s,
    loads,
    field,
    push0,
    push1,
    push_face,
    cell_s,
    owner_s,
    section_s,
    cell_v,
    owner_v,
    section_v,
    geometry,
    small_sem,
    table,
    lift_rows,
    drag_rows,
    geo0,
    geo1,
    row0,
    row1,
    rhs,
    ys1,
    yr1,
    ysp,
    yrp,
    ysm,
    yrm,
    yss,
    yrs,
    load_send,
    load_recv,
    slab_send,
    slab_recv,
    local_sem,
    polar_sem,
    x_send,
    x_recv,
    y_send,
    y_recv,
    t_send,
    t_recv,
    w_send,
    w_recv,
    l_send,
    l_recv,
    m_send,
    m_recv,
):
    sl = lax.axis_index("slab")
    se = lax.axis_index("sector")
    nx, ny, nz = pre.shape
    nj = nz // L
    slots = cell_h.shape[1]
    sec_dev = polar.shape[1]
    bins = polar.shape[2]
    has_left = sl > 0
    has_right = sl < n_slab - 1
    rows = pl.ds(PAD, ny)

    step_x = 4
    parts = nx // step_x
    order = [0, parts - 1] + list(range(1, parts - 1))

    def load(part, j):
        xs = pl.ds(part * step_x, step_x)
        xd = pl.ds(1 + part * step_x, step_x)
        zs = pl.ds(j * L, L)
        return (
            pltpu.make_async_copy(vel.at[:, xs, :, zs], field.at[0:3, xd, j, rows, :], local_sem.at[0, part, j]),
            pltpu.make_async_copy(pre.at[xs, :, zs], field.at[3, xd, j, rows, :], local_sem.at[1, part, j]),
        )

    for part in order:
        for j in range(nj):
            for c in load(part, j):
                c.start()
    polar_copies = [
        pltpu.make_async_copy(
            polar.at[:, :, pl.ds(b * L, L)], table.at[se, :, b, pl.ds(0, sec_dev), :], polar_sem.at[b]
        )
        for b in range(bins // L)
    ]
    small_copies = [
        pltpu.make_async_copy(src, dst, small_sem.at[k])
        for k, (src, dst) in enumerate(
            (
                (geometry_h, geometry),
                (cell_h, cell_s),
                (owner_h, owner_s),
                (section_h, section_s),
                (cell_h, cell_v),
                (owner_h, owner_v),
                (section_h, section_v),
            )
        )
    ]
    for c in polar_copies + small_copies:
        c.start()

    barrier = pltpu.get_barrier_semaphore()

    @pl.loop(1, n_sector)
    def _(d):
        pl.semaphore_signal(barrier, inc=1, device_id=(sl, lax.rem(se + d, n_sector)), device_id_type=MESH)

    @pl.loop(1, n_slab)
    def _(d):
        pl.semaphore_signal(barrier, inc=1, device_id=(lax.rem(sl + d, n_slab), se), device_id_type=MESH)

    def zero_plane(x):
        @pl.loop(0, nj)
        def _(j):
            for f in range(4):
                field[f, x, j, rows, :] = jnp.zeros((ny, L), F32)
            push0[x, j] = jnp.zeros((ny, L), F32)

    @pl.when(jnp.logical_not(has_left))
    def _():
        zero_plane(0)

    @pl.when(jnp.logical_not(has_right))
    def _():
        zero_plane(nx + 1)

    for c in small_copies:
        c.wait()
    load_send[...] = jnp.zeros(load_send.shape, F32)
    for c in range(2):
        for b in range(bins // L):
            table[se, c, b, sec_dev : sec_dev + 8, :] = jnp.zeros((8, L), F32)
        table[se, c, 0, sec_dev : sec_dev + 1, 0:sec_dev] = geometry[c : c + 1, :]
    for buffer in (ys1, ysp, ysm, yss):
        buffer[...] = jnp.zeros(buffer.shape, F32)
    for c in polar_copies:
        c.wait()
    pl.semaphore_wait(barrier, n_sector - 1 + n_slab - 1)

    def x_copy(stage, direction):
        kept, ghost = (1, nx + 1) if direction == 0 else (nx, 0)
        if stage == 0:
            src, dst = field.at[:, kept, :, rows, :], field.at[:, ghost, :, rows, :]
        elif stage == 1:
            src, dst = push0.at[kept], push_face.at[direction]
        else:
            src, dst = field.at[stage - 2, kept, :, rows, :], field.at[stage - 2, ghost, :, rows, :]
        return pltpu.make_async_remote_copy(
            src_ref=src,
            dst_ref=dst,
            send_sem=x_send.at[stage, direction],
            recv_sem=x_recv.at[stage, direction],
            device_id=(sl - 1 if direction == 0 else sl + 1, se),
            device_id_type=MESH,
        )

    def x_start(stage):
        @pl.when(has_left)
        def _():
            x_copy(stage, 0).start()

        @pl.when(has_right)
        def _():
            x_copy(stage, 1).start()

    def x_wait_recv(stage):
        @pl.when(has_right)
        def _():
            x_copy(stage, 0).wait_recv()

        @pl.when(has_left)
        def _():
            x_copy(stage, 1).wait_recv()

    def x_wait_send(stage):
        @pl.when(has_left)
        def _():
            x_copy(stage, 0).wait_send()

        @pl.when(has_right)
        def _():
            x_copy(stage, 1).wait_send()

    below = (sl, lax.rem(se + n_sector - 1, n_sector))
    above = (sl, lax.rem(se + 1, n_sector))

    def y_copies(slot, src, dst, at):
        return [
            pltpu.make_async_remote_copy(
                src_ref=src.at[(direction,) + at],
                dst_ref=dst.at[(direction,) + at],
                send_sem=y_send.at[slot, direction],
                recv_sem=y_recv.at[slot, direction],
                device_id=(below, above)[direction],
                device_id_type=MESH,
            )
            for direction in range(2)
        ]

    inner = (pl.ds(1, nx - 2),)
    y_all = {
        "first": y_copies(0, ys1, yr1, ()),
        "push": y_copies(1, ysp, yrp, ()),
        "mid_in": y_copies(2, ysm, yrm, inner),
        "mid_lo": y_copies(3, ysm, yrm, (0,)),
        "mid_hi": y_copies(4, ysm, yrm, (nx - 1,)),
        "set_in": y_copies(5, yss, yrs, inner),
        "set_lo": y_copies(6, yss, yrs, (0,)),
        "set_hi": y_copies(7, yss, yrs, (nx - 1,)),
    }

    def y_start(*names):
        for name in names:
            for c in y_all[name]:
                c.start()

    def y_wait_recv(*names):
        for name in names:
            for c in y_all[name]:
                c.wait_recv()

    def pack(buffer, lead, ref, lead_ref, x):
        for j in range(nj):
            buffer[(0,) + lead + (x - 1, pl.ds(j, 1))] = ref[lead_ref + (j, pl.ds(PAD, 1))]
            buffer[(1,) + lead + (x - 1, pl.ds(j, 1))] = ref[lead_ref + (j, pl.ds(PAD + ny - 1, 1))]

    def unpack(buffer, lead, ref, lead_ref, x):
        for j in range(nj):
            ref[lead_ref + (j, pl.ds(PAD + ny, 1))] = buffer[(0,) + lead + (x - 1, pl.ds(j, 1))]
            ref[lead_ref + (j, pl.ds(PAD - 1, 1))] = buffer[(1,) + lead + (x - 1, pl.ds(j, 1))]

    def table_copy(k):
        return pltpu.make_async_remote_copy(
            src_ref=table.at[se],
            dst_ref=table.at[se],
            send_sem=t_send.at[k],
            recv_sem=t_recv.at[k],
            device_id=(sl, lax.rem(se + 2 * k, n_sector)),
            device_id_type=MESH,
        )

    twin = se + 1 - 2 * lax.rem(se, 2)

    def twin_copy(k):
        block = lax.rem(se + n_sector - 2 * k, n_sector)
        return pltpu.make_async_remote_copy(
            src_ref=table.at[block],
            dst_ref=table.at[block],
            send_sem=w_send.at[k],
            recv_sem=w_recv.at[k],
            device_id=(sl, twin),
            device_id_type=MESH,
        )

    half = n_sector // 2

    for count, part in enumerate(order):
        for j in range(nj):
            for c in load(part, j):
                c.wait()
        if count == 1:
            x_start(0)

    @pl.loop(1, nx + 1)
    def _(x):
        for f in range(4):
            pack(ys1, (f,), field, (f, x), x)

    y_start("first")

    @pl.loop(1, half)
    def _(k):
        table_copy(k).start()

    twin_copy(0).start()

    lane = lax.broadcasted_iota(I32, (8, L), 1)

    def plane_of(i):
        return jnp.where(i < nx - 2, i + 2, jnp.where(i == nx - 2, 1, nx))

    y_wait_recv("first")

    @pl.loop(0, nx)
    def _(i):
        x = plane_of(i)

        @pl.when(i == nx - 2)
        def _():
            x_wait_recv(0)

        for f in range(4):
            unpack(yr1, (f,), field, (f, x), x)
        for y in range(0, ny, 8):
            here = pl.ds(PAD + y, 8)

            def sides(f, j):
                return (
                    field[f, x + 1, j, here, :],
                    field[f, x - 1, j, here, :],
                    field[f, x, j, pl.ds(PAD + y + 1, 8), :],
                    field[f, x, j, pl.ds(PAD + y - 1, 8), :],
                )

            centre = [field[3, x, j, here, :] for j in range(nj)]
            after, before = z_pair(centre, lane)
            slope = []
            for j in range(nj):
                xp, xm, yp, ym = sides(3, j)
                out_s[x - 1, pl.ds(y, 8), pl.ds(j * L, L)] = (xp + xm) + (yp + ym) + (after[j] + before[j])
                slope.append((xp - xm, yp - ym, after[j] - before[j]))
            for f in range(3):
                centre = [field[f, x, j, here, :] for j in range(nj)]
                after, before = z_pair(centre, lane)
                for j in range(nj):
                    xp, xm, yp, ym = sides(f, j)
                    total = (xp + xm) + (yp + ym) + (after[j] + before[j])
                    value = 0.4 * centre[j] + 0.1 * total - 0.25 * slope[j][f]
                    if f == 0:
                        push0[x, j, pl.ds(y, 8), :] = value
                    elif f == 1:
                        push1[x - 1, j, here, :] = value
                    else:
                        out[2, x - 1, pl.ds(y, 8), pl.ds(j * L, L)] = value

    @pl.loop(1, half)
    def _(k):
        table_copy(k).wait_recv()
        twin_copy(k).start()

    @pl.loop(0, half)
    def _(k):
        twin_copy(k).wait_recv()

    @pl.loop(0, slots, unroll=4)
    def _(s):
        cell = cell_s[0, s]
        xy = ((cell >> 8) * 21846) >> 16
        z = cell - nz * xy
        x = xy >> 6
        y = xy & (ny - 1)
        j = z >> 7
        owner = owner_s[0, s]
        section = section_s[0, s]
        at = pl.ds(s, 1)
        row0[at, :] = push0[x + 1, j, pl.ds(y, 1), :]
        row1[at, :] = push1[x, j, pl.ds(y + PAD, 1), :]
        for b in range(bins // L):
            lift_rows[b, at, :] = table[owner, 0, b, pl.ds(section, 1), :]
            drag_rows[b, at, :] = table[owner, 1, b, pl.ds(section, 1), :]
        geo0[at, :] = table[owner, 0, 0, pl.ds(sec_dev, 1), :]
        geo1[at, :] = table[owner, 1, 0, pl.ds(sec_dev, 1), :]

    diagonal = lax.broadcasted_iota(I32, (L, L), 0) == lax.broadcasted_iota(I32, (L, L), 1)
    lanes = lax.broadcasted_iota(I32, (L, L), 1).astype(F32)
    z_ids = lax.broadcasted_iota(I32, (L, nz), 1).astype(F32)
    places = lax.broadcasted_iota(I32, (L, 1), 0)
    used = count_s[0, 0]

    def column(row):
        return jnp.sum(jnp.where(diagonal, row, 0.0), axis=1, keepdims=True)

    def picked(block, lane_of):
        return jnp.sum(jnp.where(lanes == lane_of, block, 0.0), axis=1, keepdims=True)

    def xy_of(cell):
        return (((cell >> 8).astype(F32) + 0.5) * (1.0 / 3.0)).astype(I32)

    for g in range(slots // L):
        at = pl.ds(g * L, L)
        cell = cell_v[0:1, at]
        z_row = cell - nz * xy_of(cell)
        z_col = column(z_row.astype(F32))
        lane_col = column((z_row & (L - 1)).astype(F32))
        section = column(section_v[0:1, at].astype(F32))
        whole = column((owner_v[0:1, at] * sec_dev + section_v[0:1, at]).astype(F32))
        radius = 0.25 + 0.75 * (z_col + 0.5) / nz
        a = 1.0 + picked(row0[at, :], lane_col)
        t = 10.0 * radius + picked(row1[at, :], lane_col)
        chord = picked(geo0[at, :], section)
        twist = picked(geo1[at, :], section)
        position = (jnp.arctan2(a, t) - twist + 2.0) * ((bins - 1) / 4.0)
        lift, drag = 0.0, 0.0
        for b in range(bins // L):
            weight = jnp.maximum(0.0, 1.0 - jnp.abs(position - (lanes + float(b * L))))
            lift = lift + lift_rows[b, at, :] * weight
            drag = drag + drag_rows[b, at, :] * weight
        lift = jnp.sum(lift, axis=1, keepdims=True)
        drag = jnp.sum(drag, axis=1, keepdims=True)
        scale = 0.5 * chord * jnp.sqrt(a * a + t * t)
        active = places + g * L < used
        thrust = jnp.where(active, scale * (lift * t - drag * a), 0.0)
        swirl = jnp.where(active, scale * (lift * a + drag * t), 0.0)
        torque = swirl * radius
        mask = z_ids == z_col
        for c, force in ((0, 0.2 * thrust), (1, 0.2 * swirl)):
            high = force.astype(BF16).astype(F32)
            rhs[c, 0, at, :] = jnp.where(mask, high, 0.0).astype(BF16)
            rhs[c, 1, at, :] = jnp.where(mask, force - high, 0.0).astype(BF16)
        for pair in range(half):
            chosen = lanes == whole - float(pair * L)
            load_send[pair, 0:1, :] += jnp.sum(jnp.where(chosen, thrust, 0.0), axis=0, keepdims=True)
            load_send[pair, 1:2, :] += jnp.sum(jnp.where(chosen, torque, 0.0), axis=0, keepdims=True)

    def load_copy(d):
        peer = lax.rem(se + d, n_sector)
        return pltpu.make_async_remote_copy(
            src_ref=load_send.at[peer // 2],
            dst_ref=load_recv.at[se],
            send_sem=l_send.at[d],
            recv_sem=l_recv.at[d],
            device_id=(sl, peer),
            device_id_type=MESH,
        )

    def slab_copy(d):
        return pltpu.make_async_remote_copy(
            src_ref=slab_send,
            dst_ref=slab_recv.at[sl],
            send_sem=m_send.at[d],
            recv_sem=m_recv.at[d],
            device_id=(lax.rem(sl + d, n_slab), se),
            device_id_type=MESH,
        )

    chunk = 4
    high_rows = lax.broadcasted_iota(I32, (chunk * ny, slots), 0)
    xy_all = xy_of(cell_v[...])

    @pl.loop(0, nx // chunk)
    def _(i):
        m = jnp.where(i == 0, 0, jnp.where(i == 1, nx // chunk - 1, i - 1))
        chosen = jnp.where(high_rows == xy_all - m * (chunk * ny), 1.0, 0.0).astype(BF16)
        for c in range(2):
            total = jnp.dot(chosen, rhs[c, 0], preferred_element_type=F32) + jnp.dot(
                chosen, rhs[c, 1], preferred_element_type=F32
            )
            for k in range(chunk):
                for j in range(nj):
                    piece = total[k * ny : (k + 1) * ny, j * L : (j + 1) * L]
                    if c == 0:
                        push0[1 + m * chunk + k, j] += piece
                    else:
                        push1[m * chunk + k, j, rows, :] += piece

        @pl.when(i == 1)
        def _():
            x_start(1)

    @pl.loop(1, nx + 1)
    def _(x):
        pack(ysp, (), push1, (x - 1,), x)

    y_start("push")

    @pl.loop(1, n_sector)
    def _(d):
        load_copy(d).start()

    load_recv[se] = load_send[se // 2]

    y_wait_recv("push")
    x_wait_send(0)

    @pl.loop(0, nx)
    def _(i):
        x = plane_of(i)

        @pl.when(i == nx - 2)
        def _():
            y_start("mid_in")
            x_wait_recv(1)
            for direction, there, ghost in ((0, has_right, nx + 1), (1, has_left, 0)):

                @pl.when(there)
                def _():
                    for j in range(nj):
                        push0[ghost, j] = push_face[direction, j]


        unpack(yrp, (), push1, (x - 1,), x)
        for y in range(0, ny, 8):
            ys = pl.ds(y, 8)
            after, before = z_pair([out[2, x - 1, ys, pl.ds(j * L, L)] for j in range(nj)], lane)
            for j in range(nj):
                source = 0.5 * (
                    (push0[x + 1, j, ys, :] - push0[x - 1, j, ys, :])
                    + (push1[x - 1, j, pl.ds(PAD + y + 1, 8), :] - push1[x - 1, j, pl.ds(PAD + y - 1, 8), :])
                    + (after[j] - before[j])
                )
                middle = (out_s[x - 1, ys, pl.ds(j * L, L)] - source) * (1.0 / 6.0)
                field[0, x, j, pl.ds(PAD + y, 8), :] = middle
                out_s[x - 1, ys, pl.ds(j * L, L)] = source
        pack(ysm, (), field, (0, x), x)

    x_start(2)
    y_start("mid_lo", "mid_hi")

    @pl.loop(1, n_sector)
    def _(d):
        load_copy(d).wait_recv()

    mine = load_recv[0]
    for d in range(1, n_sector):
        mine = mine + load_recv[d]
    mine = jnp.where(lax.rem(se, 2) == 1, pltpu.roll(mine, L // 2, 1), mine)
    slab_send[...] = mine
    slab_recv[sl] = mine

    @pl.loop(1, n_slab)
    def _(d):
        slab_copy(d).start()

    y_wait_recv("mid_in")

    @pl.loop(0, nx)
    def _(i):
        x = plane_of(i)

        @pl.when(i == nx - 2)
        def _():
            y_start("set_in")
            y_wait_recv("mid_lo", "mid_hi")
            x_wait_recv(2)

        unpack(yrm, (), field, (0, x), x)
        for y in range(0, ny, 8):
            ys = pl.ds(y, 8)
            here = pl.ds(PAD + y, 8)
            after, before = z_pair([field[0, x, j, here, :] for j in range(nj)], lane)
            for j in range(nj):
                total = (
                    (field[0, x + 1, j, here, :] + field[0, x - 1, j, here, :])
                    + (field[0, x, j, pl.ds(PAD + y + 1, 8), :] + field[0, x, j, pl.ds(PAD + y - 1, 8), :])
                    + (after[j] + before[j])
                )
                settled = (total - out_s[x - 1, ys, pl.ds(j * L, L)]) * (1.0 / 6.0)
                field[1, x, j, here, :] = settled
                out_s[x - 1, ys, pl.ds(j * L, L)] = settled
        pack(yss, (), field, (1, x), x)

    x_start(3)
    y_start("set_lo", "set_hi")

    y_wait_recv("set_in")

    @pl.loop(0, nx)
    def _(i):
        x = plane_of(i)

        @pl.when(i == nx - 2)
        def _():
            y_wait_recv("set_lo", "set_hi")
            x_wait_recv(3)

        unpack(yrs, (), field, (1, x), x)
        for y in range(0, ny, 8):
            ys = pl.ds(y, 8)
            here = pl.ds(PAD + y, 8)
            after, before = z_pair([field[1, x, j, here, :] for j in range(nj)], lane)
            for j in range(nj):
                zs = pl.ds(j * L, L)
                out[0, x - 1, ys, zs] = push0[x, j, ys, :] - 0.5 * (field[1, x + 1, j, here, :] - field[1, x - 1, j, here, :])
                out[1, x - 1, ys, zs] = push1[x - 1, j, here, :] - 0.5 * (
                    field[1, x, j, pl.ds(PAD + y + 1, 8), :] - field[1, x, j, pl.ds(PAD + y - 1, 8), :]
                )
                out[2, x - 1, ys, zs] = out[2, x - 1, ys, zs] - 0.5 * (after[j] - before[j])

    @pl.loop(1, n_slab)
    def _(d):
        slab_copy(d).wait_recv()

    final = slab_recv[0]
    for d in range(1, n_slab):
        final = final + slab_recv[d]
    loads[...] = final[0:2, 0:sec_dev]

    for stage in range(1, 4):
        x_wait_send(stage)
    for copies in y_all.values():
        for c in copies:
            c.wait_send()

    @pl.loop(1, half)
    def _(k):
        table_copy(k).wait_send()

    @pl.loop(0, half)
    def _(k):
        twin_copy(k).wait_send()

    @pl.loop(1, n_sector)
    def _(d):
        load_copy(d).wait_send()

    @pl.loop(1, n_slab)
    def _(d):
        slab_copy(d).wait_send()


def on_device(n_slab, n_sector, velocity, pressure, disk_cell, disk_count, disk_owner, disk_section, polar, geometry):
    nx, ny, nz = pressure.shape
    nj = nz // L
    slots = disk_cell.shape[1]
    sec_dev, bins = polar.shape[1:]
    tall = ny + 2 * PAD
    owner = disk_owner.reshape(1, slots)
    dma = pltpu.SemaphoreType.DMA
    hbm = pl.BlockSpec(memory_space=pltpu.HBM)
    vmem = pl.BlockSpec(memory_space=pltpu.VMEM)
    half = n_sector // 2
    corrected, settled, loads = pl.pallas_call(
        functools.partial(kernel, n_slab, n_sector),
        out_shape=(
            pltpu.VMEM((3, nx, ny, nz), F32),
            pltpu.VMEM((nx, ny, nz), F32),
            jax.ShapeDtypeStruct((2, sec_dev), F32),
        ),
        in_specs=[hbm] * 7 + [pl.BlockSpec(memory_space=pltpu.SMEM)],
        out_specs=(vmem, vmem, vmem),
        scratch_shapes=[
            pltpu.VMEM((4, nx + 2, nj, tall, L), F32),
            pltpu.VMEM((nx + 2, nj, ny, L), F32),
            pltpu.VMEM((nx, nj, tall, L), F32),
            pltpu.VMEM((2, nj, ny, L), F32),
            pltpu.SMEM((1, slots), jnp.int32),
            pltpu.SMEM((1, slots), jnp.int32),
            pltpu.SMEM((1, slots), jnp.int32),
            pltpu.VMEM((1, slots), jnp.int32),
            pltpu.VMEM((1, slots), jnp.int32),
            pltpu.VMEM((1, slots), jnp.int32),
            pltpu.VMEM((2, sec_dev), F32),
            dma((8,)),
            pltpu.VMEM((n_sector, 2, bins // L, sec_dev + 8, L), F32),
            pltpu.VMEM((bins // L, slots, L), F32),
            pltpu.VMEM((bins // L, slots, L), F32),
            pltpu.VMEM((slots, L), F32),
            pltpu.VMEM((slots, L), F32),
            pltpu.VMEM((slots, L), F32),
            pltpu.VMEM((slots, L), F32),
            pltpu.VMEM((2, 2, slots, nz), BF16),
            pltpu.VMEM((2, 4, nx, 8, L), F32),
            pltpu.VMEM((2, 4, nx, 8, L), F32),
            pltpu.VMEM((2, nx, 8, L), F32),
            pltpu.VMEM((2, nx, 8, L), F32),
            pltpu.VMEM((2, nx, 8, L), F32),
            pltpu.VMEM((2, nx, 8, L), F32),
            pltpu.VMEM((2, nx, 8, L), F32),
            pltpu.VMEM((2, nx, 8, L), F32),
            pltpu.VMEM((half, 8, L), F32),
            pltpu.VMEM((n_sector, 8, L), F32),
            pltpu.VMEM((8, L), F32),
            pltpu.VMEM((n_slab, 8, L), F32),
            dma((2, nx // 4, nj)),
            dma((bins // L,)),
            dma((4, 2)),
            dma((4, 2)),
            dma((8, 2)),
            dma((8, 2)),
            dma((half,)),
            dma((half,)),
            dma((half,)),
            dma((half,)),
            dma((n_sector,)),
            dma((n_sector,)),
            dma((n_slab,)),
            dma((n_slab,)),
        ],
        compiler_params=pltpu.CompilerParams(
            collective_id=0, has_side_effects=True, vmem_limit_bytes=40 * 1024 * 1024
        ),
    )(
        *(
            pltpu.with_memory_space_constraint(array, pltpu.HBM)
            for array in (velocity, pressure, disk_cell, owner, disk_section, polar, geometry)
        ),
        disk_count,
    )
    return corrected, settled, loads


def solution(mesh):
    return jax.shard_map(
        functools.partial(on_device, mesh.shape["slab"], mesh.shape["sector"]),
        mesh=mesh,
        in_specs=(
            P(None, "slab", "sector", None),
            P("slab", "sector", None),
            P("slab", "sector"),
            P("slab", "sector"),
            P("slab", "sector", None),
            P("slab", "sector"),
            P(None, "sector", None),
            P(None, "sector"),
        ),
        out_specs=(P(None, "slab", "sector", None), P("slab", "sector", None), P(None, "sector")),
        check_vma=False,
    )
```

```python
import functools

import jax
import jax.numpy as jnp
from jax import lax
from jax.experimental import pallas as pl
from jax.experimental.pallas import tpu as pltpu
from jax.sharding import PartitionSpec as P

MESH = pl.DeviceIdType.MESH
F32 = jnp.float32
I32 = jnp.int32
BF16 = jnp.bfloat16
L = 128
PAD = 8


def z_pair(tiles, lane):
    up = [pltpu.roll(t, L - 1, 1) for t in tiles]
    down = [pltpu.roll(t, 1, 1) for t in tiles]
    last = len(tiles) - 1
    zero = jnp.zeros_like(tiles[0])
    after = [jnp.where(lane == L - 1, up[j + 1] if j < last else zero, up[j]) for j in range(last + 1)]
    before = [jnp.where(lane == 0, down[j - 1] if j > 0 else zero, down[j]) for j in range(last + 1)]
    return after, before


def kernel(
    n_slab,
    n_sector,
    vel,
    pre,
    cell_h,
    owner_h,
    section_h,
    polar,
    geometry_h,
    count_s,
    out,
    out_s,
    loads,
    field,
    push0,
    push1,
    x_out,
    x_in,
    cell_s,
    owner_s,
    section_s,
    cell_v,
    owner_v,
    section_v,
    geometry,
    small_sem,
    table,
    lift_rows,
    drag_rows,
    geo0,
    geo1,
    row0,
    row1,
    rhs,
    first_out,
    first_in,
    y_out,
    y_in,
    load_send,
    load_recv,
    slab_send,
    slab_recv,
    local_sem,
    polar_sem,
    x_send,
    x_recv,
    y_send,
    y_recv,
    t_send,
    t_recv,
    w_send,
    w_recv,
    l_send,
    l_recv,
    m_send,
    m_recv,
):
    sl = lax.axis_index("slab")
    se = lax.axis_index("sector")
    nx, ny, nz = pre.shape
    nj = nz // L
    slots = cell_h.shape[1]
    sec_dev = polar.shape[1]
    bins = polar.shape[2]
    has_left = sl > 0
    has_right = sl < n_slab - 1
    rows = pl.ds(PAD, ny)

    parts = ((0, 1), (nx - 1, 1), (1, nx // 2 - 1), (nx // 2, nx // 2 - 1))

    def load(part, j):
        start, count = parts[part]
        xs = pl.ds(start, count)
        xd = pl.ds(1 + start, count)
        zs = pl.ds(j * L, L)
        return (
            pltpu.make_async_copy(vel.at[:, xs, :, zs], field.at[0:3, xd, j, rows, :], local_sem.at[0, part, j]),
            pltpu.make_async_copy(pre.at[xs, :, zs], field.at[3, xd, j, rows, :], local_sem.at[1, part, j]),
        )

    for part in range(len(parts)):
        for j in range(nj):
            for c in load(part, j):
                c.start()
    polar_copies = [
        pltpu.make_async_copy(
            polar.at[:, :, pl.ds(b * L, L)], table.at[se, :, b, pl.ds(0, sec_dev), :], polar_sem.at[b]
        )
        for b in range(bins // L)
    ]
    small_copies = [
        pltpu.make_async_copy(src, dst, small_sem.at[k])
        for k, (src, dst) in enumerate(
            (
                (geometry_h, geometry),
                (cell_h, cell_s),
                (owner_h, owner_s),
                (section_h, section_s),
                (cell_h, cell_v),
                (owner_h, owner_v),
                (section_h, section_v),
            )
        )
    ]
    for c in polar_copies + small_copies:
        c.start()

    barrier = pltpu.get_barrier_semaphore()

    @pl.loop(1, n_sector)
    def _(d):
        pl.semaphore_signal(barrier, inc=1, device_id=(sl, lax.rem(se + d, n_sector)), device_id_type=MESH)

    @pl.loop(1, n_slab)
    def _(d):
        pl.semaphore_signal(barrier, inc=1, device_id=(lax.rem(sl + d, n_slab), se), device_id_type=MESH)

    @pl.loop(1, nx + 1)
    def _(x):
        for beyond in (0, PAD + ny):
            for j in range(nj):
                for f in range(4):
                    field[f, x, j, beyond : beyond + PAD, :] = jnp.zeros((PAD, L), F32)
                push1[x - 1, j, beyond : beyond + PAD, :] = jnp.zeros((PAD, L), F32)

    for ghost in (0, nx + 1):

        @pl.loop(0, nj)
        def _(j):
            for f in range(4):
                field[f, ghost, j, rows, :] = jnp.zeros((ny, L), F32)
            push0[ghost, j] = jnp.zeros((ny, L), F32)

    for c in small_copies:
        c.wait()
    load_send[...] = jnp.zeros(load_send.shape, F32)
    for c in range(2):
        for b in range(bins // L):
            table[se, c, b, sec_dev : sec_dev + 8, :] = jnp.zeros((8, L), F32)
        table[se, c, 0, sec_dev : sec_dev + 1, 0:sec_dev] = geometry[c : c + 1, :]
    for buffer in (first_out, y_out):
        buffer[...] = jnp.zeros(buffer.shape, F32)
    W0, V1, V2, MID, SET, COR = range(6)

    def x_copy(stage, direction):
        kept = 1 if direction == 0 else nx
        if stage in (V1, V2):
            src = field.at[stage, kept, :, rows, :]
        elif stage == COR:
            src = field.at[1, kept, :, rows, :]
        else:
            src = x_out.at[{W0: 0, MID: 1, SET: 2}[stage], direction]
        return pltpu.make_async_remote_copy(
            src_ref=src,
            dst_ref=x_in.at[stage, direction],
            send_sem=x_send.at[stage, direction],
            recv_sem=x_recv.at[stage, direction],
            device_id=(sl - 1 if direction == 0 else sl + 1, se),
            device_id_type=MESH,
        )

    def x_faces(body):
        for direction, there, kept in ((0, has_right, nx), (1, has_left, 1)):

            @pl.when(there)
            def _():
                @pl.loop(0, nj)
                def _(j):
                    body(direction, kept, j)

    def x_start(stage):
        @pl.when(has_left)
        def _():
            x_copy(stage, 0).start()

        @pl.when(has_right)
        def _():
            x_copy(stage, 1).start()

    def x_wait_recv(stage):
        @pl.when(has_right)
        def _():
            x_copy(stage, 0).wait_recv()

        @pl.when(has_left)
        def _():
            x_copy(stage, 1).wait_recv()

    def x_wait_send(stage):
        @pl.when(has_left)
        def _():
            x_copy(stage, 0).wait_send()

        @pl.when(has_right)
        def _():
            x_copy(stage, 1).wait_send()

    below = (sl, lax.rem(se + n_sector - 1, n_sector))
    above = (sl, lax.rem(se + 1, n_sector))

    def y_copies(stage):
        return [
            pltpu.make_async_remote_copy(
                src_ref=first_out.at[direction] if stage == 0 else y_out.at[stage - 1, direction],
                dst_ref=first_in.at[direction] if stage == 0 else y_in.at[stage - 1, direction],
                send_sem=y_send.at[stage, direction],
                recv_sem=y_recv.at[stage, direction],
                device_id=(below, above)[direction],
                device_id_type=MESH,
            )
            for direction in range(2)
        ]

    y_all = [y_copies(stage) for stage in range(4)]

    def y_start(stage):
        for c in y_all[stage]:
            c.start()

    def y_wait_recv(stage):
        for c in y_all[stage]:
            c.wait_recv()

    edges = ((0, 0, -1.0), (1, ny - 1, 1.0))
    far_edges = ((0, ny - 1, -1.0), (1, 0, 1.0))

    def y_rows(places, body):
        @pl.loop(1, nx + 1)
        def _(x):
            for j in range(nj):
                for direction, y, sign in places:
                    body(direction, y, sign, x, j)

    core = lax.rem(se, 2)
    tall_z = n_sector // 4
    z_here = lax.rem(se // 2, tall_z)
    y_here = se // (2 * tall_z)

    def at_step(dy, dz):
        return lax.rem(y_here + dy, 2) * (2 * tall_z) + lax.rem(z_here + dz, tall_z) * 2 + core

    down, up = tall_z - 1, 1
    relay_from = down + (up - down) * core
    relay_to = up + (down - up) * core

    def table_copy(k):
        block, target = (
            ((0, 0), (1, 0)),
            ((0, 0), (0, up)),
            ((0, 0), (0, down)),
            ((1, 0), (0, up)),
            ((1, 0), (0, down)),
            ((0, relay_from), (0, relay_to)),
            ((1, relay_from), (0, relay_to)),
        )[k]
        return pltpu.make_async_remote_copy(
            src_ref=table.at[at_step(*block)],
            dst_ref=table.at[at_step(*block)],
            send_sem=t_send.at[k],
            recv_sem=t_recv.at[k],
            device_id=(sl, at_step(*target)),
            device_id_type=MESH,
        )

    twin = se + 1 - 2 * core

    def twin_copy(dy, dz):
        return pltpu.make_async_remote_copy(
            src_ref=table.at[at_step(dy, dz)],
            dst_ref=table.at[at_step(dy, dz)],
            send_sem=w_send.at[dy * tall_z + dz],
            recv_sem=w_recv.at[dy * tall_z + dz],
            device_id=(sl, twin),
            device_id_type=MESH,
        )

    twins = [twin_copy(dy, dz) for dy in range(2) for dz in range(tall_z)]

    half = n_sector // 2

    def wait_part(part):
        for j in range(nj):
            for c in load(part, j):
                c.wait()

    wait_part(0)
    wait_part(1)

    @pl.loop(0, nj)
    def _(j):
        for direction, kept, sign in ((0, 1, -0.25), (1, nx, 0.25)):
            x_out[0, direction, j] = 0.1 * field[0, kept, j, rows, :] + sign * field[3, kept, j, rows, :]

    pl.semaphore_wait(barrier, n_sector - 1 + n_slab - 1)
    x_start(W0)
    x_start(V1)
    for c in polar_copies:
        c.wait()
    for k in range(3):
        table_copy(k).start()
    twin_copy(0, 0).start()
    wait_part(2)
    wait_part(3)

    def pack_first(direction, y, sign, x, j):
        at = pl.ds(PAD + y, 1)
        to = (x - 1, pl.ds(j, 1))
        first_out[(direction, 0) + to] = 0.1 * field[0, x, j, at, :]
        first_out[(direction, 1) + to] = 0.1 * field[1, x, j, at, :] + (0.25 * sign) * field[3, x, j, at, :]
        first_out[(direction, 2) + to] = 0.1 * field[2, x, j, at, :]

    y_rows(edges, pack_first)
    y_start(0)

    lane = lax.broadcasted_iota(I32, (8, L), 1)

    @pl.loop(1, nx + 1)
    def _(x):
        @pl.when(x == nx // 2 + 1)
        def _():
            table_copy(1).wait_recv()
            table_copy(2).wait_recv()
            table_copy(5).start()
            twin_copy(0, up).start()
            twin_copy(0, down).start()

        @pl.when(x == nx // 2 + 4)
        def _():
            table_copy(0).wait_recv()
            table_copy(3).start()
            table_copy(4).start()
            twin_copy(1, 0).start()

        for y in range(0, ny, 8):
            here = pl.ds(PAD + y, 8)

            def sides(f, j):
                return (
                    field[f, x + 1, j, here, :],
                    field[f, x - 1, j, here, :],
                    field[f, x, j, pl.ds(PAD + y + 1, 8), :],
                    field[f, x, j, pl.ds(PAD + y - 1, 8), :],
                )

            centre = [field[3, x, j, here, :] for j in range(nj)]
            after, before = z_pair(centre, lane)
            slope = []
            for j in range(nj):
                xp, xm, yp, ym = sides(3, j)
                out_s[x - 1, pl.ds(y, 8), pl.ds(j * L, L)] = (xp + xm) + (yp + ym) + (after[j] + before[j])
                slope.append((xp - xm, yp - ym, after[j] - before[j]))
            for f in range(3):
                centre = [field[f, x, j, here, :] for j in range(nj)]
                after, before = z_pair(centre, lane)
                for j in range(nj):
                    xp, xm, yp, ym = sides(f, j)
                    total = (xp + xm) + (yp + ym) + (after[j] + before[j])
                    value = 0.4 * centre[j] + 0.1 * total - 0.25 * slope[j][f]
                    if f == 0:
                        push0[x, j, pl.ds(y, 8), :] = value
                    elif f == 1:
                        push1[x - 1, j, here, :] = value
                    else:
                        out[2, x - 1, pl.ds(y, 8), pl.ds(j * L, L)] = value

    table_copy(5).wait_recv()
    twin_copy(0, 2).start()
    table_copy(3).wait_recv()
    table_copy(4).wait_recv()
    table_copy(6).start()
    twin_copy(1, up).start()
    twin_copy(1, down).start()
    x_wait_recv(W0)
    x_wait_recv(V1)
    x_start(V2)
    y_wait_recv(0)

    def add_first(direction, kept, j):
        push0[kept, j] += x_in[W0, direction, j]
        push1[kept - 1, j, rows, :] += 0.1 * x_in[V1, direction, j]

    x_faces(add_first)

    def add_first_rows(direction, y, sign, x, j):
        at = (x - 1, pl.ds(j, 1))
        push0[x, j, pl.ds(y, 1), :] += first_in[(direction, 0) + at]
        push1[x - 1, j, pl.ds(PAD + y, 1), :] += first_in[(direction, 1) + at]
        out[2, x - 1, pl.ds(y, 1), pl.ds(j * L, L)] += first_in[(direction, 2) + at]

    y_rows(far_edges, add_first_rows)

    @pl.loop(0, slots, unroll=4)
    def _(s):
        cell = cell_s[0, s]
        xy = ((cell >> 8) * 21846) >> 16
        z = cell - nz * xy
        x = xy >> 6
        y = xy & (ny - 1)
        j = z >> 7
        at = pl.ds(s, 1)
        row0[at, :] = push0[x + 1, j, pl.ds(y, 1), :]
        row1[at, :] = push1[x, j, pl.ds(y + PAD, 1), :]

    table_copy(6).wait_recv()
    twin_copy(1, 2).start()
    for c in twins:
        c.wait_recv()

    @pl.loop(0, slots, unroll=4)
    def _(s):
        owner = owner_s[0, s]
        section = section_s[0, s]
        at = pl.ds(s, 1)
        for b in range(bins // L):
            lift_rows[b, at, :] = table[owner, 0, b, pl.ds(section, 1), :]
            drag_rows[b, at, :] = table[owner, 1, b, pl.ds(section, 1), :]
        geo0[at, :] = table[owner, 0, 0, pl.ds(sec_dev, 1), :]
        geo1[at, :] = table[owner, 1, 0, pl.ds(sec_dev, 1), :]

    diagonal = lax.broadcasted_iota(I32, (L, L), 0) == lax.broadcasted_iota(I32, (L, L), 1)
    lanes = lax.broadcasted_iota(I32, (L, L), 1).astype(F32)
    z_ids = lax.broadcasted_iota(I32, (L, nz), 1).astype(F32)
    places = lax.broadcasted_iota(I32, (L, 1), 0)
    used = count_s[0, 0]

    def column(row):
        return jnp.sum(jnp.where(diagonal, row, 0.0), axis=1, keepdims=True)

    def picked(block, lane_of):
        return jnp.sum(jnp.where(lanes == lane_of, block, 0.0), axis=1, keepdims=True)

    def xy_of(cell):
        return (((cell >> 8).astype(F32) + 0.5) * (1.0 / 3.0)).astype(I32)

    for g in range(slots // L):
        at = pl.ds(g * L, L)
        cell = cell_v[0:1, at]
        z_row = cell - nz * xy_of(cell)
        z_col = column(z_row.astype(F32))
        lane_col = column((z_row & (L - 1)).astype(F32))
        section = column(section_v[0:1, at].astype(F32))
        whole = column((owner_v[0:1, at] * sec_dev + section_v[0:1, at]).astype(F32))
        radius = 0.25 + 0.75 * (z_col + 0.5) / nz
        a = 1.0 + picked(row0[at, :], lane_col)
        t = 10.0 * radius + picked(row1[at, :], lane_col)
        chord = picked(geo0[at, :], section)
        twist = picked(geo1[at, :], section)
        position = (jnp.arctan2(a, t) - twist + 2.0) * ((bins - 1) / 4.0)
        lift, drag = 0.0, 0.0
        for b in range(bins // L):
            weight = jnp.maximum(0.0, 1.0 - jnp.abs(position - (lanes + float(b * L))))
            lift = lift + lift_rows[b, at, :] * weight
            drag = drag + drag_rows[b, at, :] * weight
        lift = jnp.sum(lift, axis=1, keepdims=True)
        drag = jnp.sum(drag, axis=1, keepdims=True)
        scale = 0.5 * chord * jnp.sqrt(a * a + t * t)
        active = places + g * L < used
        thrust = jnp.where(active, scale * (lift * t - drag * a), 0.0)
        swirl = jnp.where(active, scale * (lift * a + drag * t), 0.0)
        torque = swirl * radius
        mask = z_ids == z_col
        for c, force in ((0, 0.2 * thrust), (1, 0.2 * swirl)):
            high = force.astype(BF16).astype(F32)
            rhs[c, 0, at, :] = jnp.where(mask, high, 0.0).astype(BF16)
            rhs[c, 1, at, :] = jnp.where(mask, force - high, 0.0).astype(BF16)
        for pair in range(half):
            chosen = lanes == whole - float(pair * L)
            load_send[pair, 0:1, :] += jnp.sum(jnp.where(chosen, thrust, 0.0), axis=0, keepdims=True)
            load_send[pair, 1:2, :] += jnp.sum(jnp.where(chosen, torque, 0.0), axis=0, keepdims=True)

    def load_copy(d):
        peer = lax.rem(se + d, n_sector)
        return pltpu.make_async_remote_copy(
            src_ref=load_send.at[peer // 2],
            dst_ref=load_recv.at[se],
            send_sem=l_send.at[d],
            recv_sem=l_recv.at[d],
            device_id=(sl, peer),
            device_id_type=MESH,
        )

    def slab_copy(d):
        return pltpu.make_async_remote_copy(
            src_ref=slab_send,
            dst_ref=slab_recv.at[sl],
            send_sem=m_send.at[d],
            recv_sem=m_recv.at[d],
            device_id=(lax.rem(sl + d, n_slab), se),
            device_id_type=MESH,
        )

    chunk = 4
    high_rows = lax.broadcasted_iota(I32, (chunk * ny, slots), 0)
    xy_all = xy_of(cell_v[...])

    @pl.loop(0, nx // chunk)
    def _(i):
        m = jnp.where(i == 0, 0, jnp.where(i == 1, nx // chunk - 1, i - 1))
        chosen = jnp.where(high_rows == xy_all - m * (chunk * ny), 1.0, 0.0).astype(BF16)
        for c in range(2):
            total = jnp.dot(chosen, rhs[c, 0], preferred_element_type=F32) + jnp.dot(
                chosen, rhs[c, 1], preferred_element_type=F32
            )
            for k in range(chunk):
                for j in range(nj):
                    piece = total[k * ny : (k + 1) * ny, j * L : (j + 1) * L]
                    if c == 0:
                        push0[1 + m * chunk + k, j] += piece
                    else:
                        push1[m * chunk + k, j, rows, :] += piece

        @pl.when(i == 1)
        def _():
            @pl.loop(0, nj)
            def _(j):
                for direction, kept, sign in ((0, 1, -0.5), (1, nx, 0.5)):
                    x_out[1, direction, j] = field[3, kept, j, rows, :] + sign * push0[kept, j]

            x_start(MID)

    def pack_middle(direction, y, sign, x, j):
        at = pl.ds(PAD + y, 1)
        y_out[0, direction, x - 1, pl.ds(j, 1)] = field[3, x, j, at, :] + (0.5 * sign) * push1[x - 1, j, at, :]

    y_rows(edges, pack_middle)
    y_start(1)

    @pl.loop(1, n_sector)
    def _(d):
        load_copy(d).start()

    load_recv[se] = load_send[se // 2]

    x_wait_recv(V2)

    def add_depth(direction, kept, j):
        for k in range(nj):

            @pl.when(j == k)
            def _():
                out[2, kept - 1, :, pl.ds(k * L, L)] += 0.1 * x_in[V2, direction, k]

    x_faces(add_depth)

    @pl.loop(1, nx + 1)
    def _(x):
        for y in range(0, ny, 8):
            ys = pl.ds(y, 8)
            after, before = z_pair([out[2, x - 1, ys, pl.ds(j * L, L)] for j in range(nj)], lane)
            for j in range(nj):
                source = 0.5 * (
                    (push0[x + 1, j, ys, :] - push0[x - 1, j, ys, :])
                    + (push1[x - 1, j, pl.ds(PAD + y + 1, 8), :] - push1[x - 1, j, pl.ds(PAD + y - 1, 8), :])
                    + (after[j] - before[j])
                )
                middle = (out_s[x - 1, ys, pl.ds(j * L, L)] - source) * (1.0 / 6.0)
                field[0, x, j, pl.ds(PAD + y, 8), :] = middle
                out_s[x - 1, ys, pl.ds(j * L, L)] = source

    x_wait_recv(MID)
    y_wait_recv(1)

    def add_middle(direction, kept, j):
        field[0, kept, j, rows, :] += (1.0 / 6.0) * x_in[MID, direction, j]

    x_faces(add_middle)

    def add_middle_rows(direction, y, sign, x, j):
        field[0, x, j, pl.ds(PAD + y, 1), :] += (1.0 / 6.0) * y_in[0, direction, x - 1, pl.ds(j, 1)]

    y_rows(far_edges, add_middle_rows)

    @pl.loop(0, nj)
    def _(j):
        for direction, kept, sign in ((0, 1, -0.5), (1, nx, 0.5)):
            x_out[2, direction, j] = field[0, kept, j, rows, :] + sign * push0[kept, j]

    x_start(SET)

    def pack_settled(direction, y, sign, x, j):
        at = pl.ds(PAD + y, 1)
        y_out[1, direction, x - 1, pl.ds(j, 1)] = field[0, x, j, at, :] + (0.5 * sign) * push1[x - 1, j, at, :]

    y_rows(edges, pack_settled)
    y_start(2)

    @pl.loop(1, n_sector)
    def _(d):
        load_copy(d).wait_recv()

    mine = load_recv[0]
    for d in range(1, n_sector):
        mine = mine + load_recv[d]
    mine = jnp.where(lax.rem(se, 2) == 1, pltpu.roll(mine, L // 2, 1), mine)
    slab_send[...] = mine
    slab_recv[sl] = mine

    @pl.loop(1, n_slab)
    def _(d):
        slab_copy(d).start()

    x_wait_send(V1)

    @pl.loop(1, nx + 1)
    def _(x):
        for y in range(0, ny, 8):
            ys = pl.ds(y, 8)
            here = pl.ds(PAD + y, 8)
            after, before = z_pair([field[0, x, j, here, :] for j in range(nj)], lane)
            for j in range(nj):
                total = (
                    (field[0, x + 1, j, here, :] + field[0, x - 1, j, here, :])
                    + (field[0, x, j, pl.ds(PAD + y + 1, 8), :] + field[0, x, j, pl.ds(PAD + y - 1, 8), :])
                    + (after[j] + before[j])
                )
                settled = (total - out_s[x - 1, ys, pl.ds(j * L, L)]) * (1.0 / 6.0)
                field[1, x, j, here, :] = settled

    x_wait_recv(SET)
    y_wait_recv(2)

    def add_settled(direction, kept, j):
        field[1, kept, j, rows, :] += (1.0 / 6.0) * x_in[SET, direction, j]

    x_faces(add_settled)

    def add_settled_rows(direction, y, sign, x, j):
        field[1, x, j, pl.ds(PAD + y, 1), :] += (1.0 / 6.0) * y_in[1, direction, x - 1, pl.ds(j, 1)]

    y_rows(far_edges, add_settled_rows)
    x_start(COR)

    def pack_corrected(direction, y, sign, x, j):
        y_out[2, direction, x - 1, pl.ds(j, 1)] = field[1, x, j, pl.ds(PAD + y, 1), :]

    y_rows(edges, pack_corrected)
    y_start(3)

    @pl.loop(1, nx + 1)
    def _(x):
        for y in range(0, ny, 8):
            ys = pl.ds(y, 8)
            here = pl.ds(PAD + y, 8)
            centre = [field[1, x, j, here, :] for j in range(nj)]
            after, before = z_pair(centre, lane)
            for j in range(nj):
                zs = pl.ds(j * L, L)
                out_s[x - 1, ys, zs] = centre[j]
                out[0, x - 1, ys, zs] = push0[x, j, ys, :] - 0.5 * (field[1, x + 1, j, here, :] - field[1, x - 1, j, here, :])
                out[1, x - 1, ys, zs] = push1[x - 1, j, here, :] - 0.5 * (
                    field[1, x, j, pl.ds(PAD + y + 1, 8), :] - field[1, x, j, pl.ds(PAD + y - 1, 8), :]
                )
                out[2, x - 1, ys, zs] = out[2, x - 1, ys, zs] - 0.5 * (after[j] - before[j])

    x_wait_recv(COR)
    for direction, there, kept, sign in ((0, has_right, nx, -0.5), (1, has_left, 1, 0.5)):

        @pl.when(there)
        def _():
            for j in range(nj):
                out[0, kept - 1, :, pl.ds(j * L, L)] += sign * x_in[COR, direction, j]

    y_wait_recv(3)

    def add_corrected_rows(direction, y, sign, x, j):
        out[1, x - 1, pl.ds(y, 1), pl.ds(j * L, L)] += (0.5 * sign) * y_in[2, direction, x - 1, pl.ds(j, 1)]

    y_rows(far_edges, add_corrected_rows)

    @pl.loop(1, n_slab)
    def _(d):
        slab_copy(d).wait_recv()

    final = slab_recv[0]
    for d in range(1, n_slab):
        final = final + slab_recv[d]
    loads[...] = final[0:2, 0:sec_dev]

    for stage in (W0, V2, MID, SET, COR):
        x_wait_send(stage)
    for copies in y_all:
        for c in copies:
            c.wait_send()

    for k in range(7):
        table_copy(k).wait_send()
    for c in twins:
        c.wait_send()

    @pl.loop(1, n_sector)
    def _(d):
        load_copy(d).wait_send()

    @pl.loop(1, n_slab)
    def _(d):
        slab_copy(d).wait_send()


def on_device(n_slab, n_sector, velocity, pressure, disk_cell, disk_count, disk_owner, disk_section, polar, geometry):
    nx, ny, nz = pressure.shape
    nj = nz // L
    slots = disk_cell.shape[1]
    sec_dev, bins = polar.shape[1:]
    tall = ny + 2 * PAD
    owner = disk_owner.reshape(1, slots)
    dma = pltpu.SemaphoreType.DMA
    hbm = pl.BlockSpec(memory_space=pltpu.HBM)
    vmem = pl.BlockSpec(memory_space=pltpu.VMEM)
    half = n_sector // 2
    corrected, settled, loads = pl.pallas_call(
        functools.partial(kernel, n_slab, n_sector),
        out_shape=(
            pltpu.VMEM((3, nx, ny, nz), F32),
            pltpu.VMEM((nx, ny, nz), F32),
            jax.ShapeDtypeStruct((2, sec_dev), F32),
        ),
        in_specs=[hbm] * 7 + [pl.BlockSpec(memory_space=pltpu.SMEM)],
        out_specs=(vmem, vmem, vmem),
        scratch_shapes=[
            pltpu.VMEM((4, nx + 2, nj, tall, L), F32),
            pltpu.VMEM((nx + 2, nj, ny, L), F32),
            pltpu.VMEM((nx, nj, tall, L), F32),
            pltpu.VMEM((3, 2, nj, ny, L), F32),
            pltpu.VMEM((6, 2, nj, ny, L), F32),
            pltpu.SMEM((1, slots), jnp.int32),
            pltpu.SMEM((1, slots), jnp.int32),
            pltpu.SMEM((1, slots), jnp.int32),
            pltpu.VMEM((1, slots), jnp.int32),
            pltpu.VMEM((1, slots), jnp.int32),
            pltpu.VMEM((1, slots), jnp.int32),
            pltpu.VMEM((2, sec_dev), F32),
            dma((8,)),
            pltpu.VMEM((n_sector, 2, bins // L, sec_dev + 8, L), F32),
            pltpu.VMEM((bins // L, slots, L), F32),
            pltpu.VMEM((bins // L, slots, L), F32),
            pltpu.VMEM((slots, L), F32),
            pltpu.VMEM((slots, L), F32),
            pltpu.VMEM((slots, L), F32),
            pltpu.VMEM((slots, L), F32),
            pltpu.VMEM((2, 2, slots, nz), BF16),
            pltpu.VMEM((2, 3, nx, 8, L), F32),
            pltpu.VMEM((2, 3, nx, 8, L), F32),
            pltpu.VMEM((3, 2, nx, 8, L), F32),
            pltpu.VMEM((3, 2, nx, 8, L), F32),
            pltpu.VMEM((half, 8, L), F32),
            pltpu.VMEM((n_sector, 8, L), F32),
            pltpu.VMEM((8, L), F32),
            pltpu.VMEM((n_slab, 8, L), F32),
            dma((2, 4, nj)),
            dma((bins // L,)),
            dma((6, 2)),
            dma((6, 2)),
            dma((4, 2)),
            dma((4, 2)),
            dma((half,)),
            dma((half,)),
            dma((half,)),
            dma((half,)),
            dma((n_sector,)),
            dma((n_sector,)),
            dma((n_slab,)),
            dma((n_slab,)),
        ],
        compiler_params=pltpu.CompilerParams(
            collective_id=0, has_side_effects=True, vmem_limit_bytes=40 * 1024 * 1024
        ),
    )(
        *(
            pltpu.with_memory_space_constraint(array, pltpu.HBM)
            for array in (velocity, pressure, disk_cell, owner, disk_section, polar, geometry)
        ),
        disk_count,
    )
    return corrected, settled, loads


def solution(mesh):
    return jax.shard_map(
        functools.partial(on_device, mesh.shape["slab"], mesh.shape["sector"]),
        mesh=mesh,
        in_specs=(
            P(None, "slab", "sector", None),
            P("slab", "sector", None),
            P("slab", "sector"),
            P("slab", "sector"),
            P("slab", "sector", None),
            P("slab", "sector"),
            P(None, "sector", None),
            P(None, "sector"),
        ),
        out_specs=(P(None, "slab", "sector", None), P("slab", "sector", None), P(None, "sector")),
        check_vma=False,
    )
```

```python
import functools

import jax
import jax.numpy as jnp
from jax import lax
from jax.experimental import pallas as pl
from jax.experimental.pallas import tpu as pltpu
from jax.sharding import PartitionSpec as P

MESH = pl.DeviceIdType.MESH
F32 = jnp.float32
I32 = jnp.int32
BF16 = jnp.bfloat16
L = 128
PAD = 8


def z_pair(tiles, lane):
    up = [pltpu.roll(t, L - 1, 1) for t in tiles]
    down = [pltpu.roll(t, 1, 1) for t in tiles]
    last = len(tiles) - 1
    zero = jnp.zeros_like(tiles[0])
    after = [jnp.where(lane == L - 1, up[j + 1] if j < last else zero, up[j]) for j in range(last + 1)]
    before = [jnp.where(lane == 0, down[j - 1] if j > 0 else zero, down[j]) for j in range(last + 1)]
    return after, before


def kernel(
    n_slab,
    n_sector,
    vel,
    pre,
    cell_h,
    owner_h,
    section_h,
    polar,
    geometry_h,
    count_s,
    out,
    out_s,
    loads,
    field,
    push0,
    push1,
    x_out,
    x_in,
    cell_s,
    owner_s,
    section_s,
    cell_v,
    owner_v,
    section_v,
    geometry,
    small_sem,
    table,
    lift_rows,
    drag_rows,
    geo0,
    geo1,
    row0,
    row1,
    rhs,
    first_out,
    first_in,
    y_out,
    y_in,
    load_send,
    load_recv,
    slab_send,
    slab_recv,
    local_sem,
    polar_sem,
    x_send,
    x_recv,
    y_send,
    y_recv,
    t_send,
    t_recv,
    w_send,
    w_recv,
    l_send,
    l_recv,
    m_send,
    m_recv,
):
    sl = lax.axis_index("slab")
    se = lax.axis_index("sector")
    nx, ny, nz = pre.shape
    nj = nz // L
    slots = cell_h.shape[1]
    sec_dev = polar.shape[1]
    bins = polar.shape[2]
    has_left = sl > 0
    has_right = sl < n_slab - 1
    rows = pl.ds(PAD, ny)

    parts = ((0, 1), (nx - 1, 1), (1, nx // 2 - 1), (nx // 2, nx // 2 - 1))

    def load(part, j):
        start, count = parts[part]
        xs = pl.ds(start, count)
        xd = pl.ds(1 + start, count)
        zs = pl.ds(j * L, L)
        return (
            pltpu.make_async_copy(vel.at[:, xs, :, zs], field.at[0:3, xd, j, rows, :], local_sem.at[0, part, j]),
            pltpu.make_async_copy(pre.at[xs, :, zs], field.at[3, xd, j, rows, :], local_sem.at[1, part, j]),
        )

    for part in range(len(parts)):
        for j in range(nj):
            for c in load(part, j):
                c.start()
    polar_copies = [
        pltpu.make_async_copy(
            polar.at[:, :, pl.ds(b * L, L)], table.at[se, :, b, pl.ds(0, sec_dev), :], polar_sem.at[b]
        )
        for b in range(bins // L)
    ]
    small_copies = [
        pltpu.make_async_copy(src, dst, small_sem.at[k])
        for k, (src, dst) in enumerate(
            (
                (geometry_h, geometry),
                (cell_h, cell_s),
                (owner_h, owner_s),
                (section_h, section_s),
                (cell_h, cell_v),
                (owner_h, owner_v),
                (section_h, section_v),
            )
        )
    ]
    for c in polar_copies + small_copies:
        c.start()

    barrier = pltpu.get_barrier_semaphore()

    @pl.loop(1, n_sector)
    def _(d):
        pl.semaphore_signal(barrier, inc=1, device_id=(sl, lax.rem(se + d, n_sector)), device_id_type=MESH)

    @pl.loop(1, n_slab)
    def _(d):
        pl.semaphore_signal(barrier, inc=1, device_id=(lax.rem(sl + d, n_slab), se), device_id_type=MESH)

    @pl.loop(1, nx + 1)
    def _(x):
        for beyond in (0, PAD + ny):
            for j in range(nj):
                for f in range(4):
                    field[f, x, j, beyond : beyond + PAD, :] = jnp.zeros((PAD, L), F32)
                push1[x - 1, j, beyond : beyond + PAD, :] = jnp.zeros((PAD, L), F32)

    for ghost in (0, nx + 1):

        @pl.loop(0, nj)
        def _(j):
            for f in range(4):
                field[f, ghost, j, rows, :] = jnp.zeros((ny, L), F32)
            push0[ghost, j] = jnp.zeros((ny, L), F32)

    for c in small_copies:
        c.wait()
    load_send[...] = jnp.zeros(load_send.shape, F32)
    for c in range(2):
        for b in range(bins // L):
            table[se, c, b, sec_dev : sec_dev + 8, :] = jnp.zeros((8, L), F32)
        table[se, c, 0, sec_dev : sec_dev + 1, 0:sec_dev] = geometry[c : c + 1, :]
    for buffer in (first_out, y_out):
        buffer[...] = jnp.zeros(buffer.shape, F32)
    W0, V1, V2, MID, SET, COR = range(6)

    halves = (0, 1)
    deep = nj // 2

    def x_copy(stage, direction, h):
        kept = 1 if direction == 0 else nx
        js = pl.ds(h * deep, deep)
        if stage in (V1, V2):
            src = field.at[stage, kept, js, rows, :]
        elif stage == COR:
            src = field.at[1, kept, js, rows, :]
        else:
            src = x_out.at[{W0: 0, MID: 1, SET: 2}[stage], direction, js]
        return pltpu.make_async_remote_copy(
            src_ref=src,
            dst_ref=x_in.at[stage, direction, js],
            send_sem=x_send.at[stage, direction, h],
            recv_sem=x_recv.at[stage, direction, h],
            device_id=(sl - 1 if direction == 0 else sl + 1, se),
            device_id_type=MESH,
        )

    def x_faces(body, h=None):
        for direction, there, kept in ((0, has_right, nx), (1, has_left, 1)):

            @pl.when(there)
            def _():
                for j in range(nj) if h is None else range(h * deep, (h + 1) * deep):
                    body(direction, kept, j)

    def x_each(act, sending, stage, parts):
        for h in parts:
            for direction, there in ((0, has_left if sending else has_right), (1, has_right if sending else has_left)):

                @pl.when(there)
                def _():
                    act(x_copy(stage, direction, h))

    def x_start(stage, parts=halves):
        x_each(lambda c: c.start(), True, stage, parts)

    def x_wait_recv(stage, parts=halves):
        x_each(lambda c: c.wait_recv(), False, stage, parts)

    def x_wait_send(stage):
        x_each(lambda c: c.wait_send(), True, stage, halves)

    below = (sl, lax.rem(se + n_sector - 1, n_sector))
    above = (sl, lax.rem(se + 1, n_sector))

    def y_copies(stage):
        return [
            pltpu.make_async_remote_copy(
                src_ref=first_out.at[direction] if stage == 0 else y_out.at[stage - 1, direction],
                dst_ref=first_in.at[direction] if stage == 0 else y_in.at[stage - 1, direction],
                send_sem=y_send.at[stage, direction],
                recv_sem=y_recv.at[stage, direction],
                device_id=(below, above)[direction],
                device_id_type=MESH,
            )
            for direction in range(2)
        ]

    y_all = [y_copies(stage) for stage in range(4)]

    def y_start(stage):
        for c in y_all[stage]:
            c.start()

    def y_wait_recv(stage):
        for c in y_all[stage]:
            c.wait_recv()

    edges = ((0, 0, -1.0), (1, ny - 1, 1.0))
    far_edges = ((0, ny - 1, -1.0), (1, 0, 1.0))

    def y_rows(places, body):
        @pl.loop(1, nx + 1)
        def _(x):
            for j in range(nj):
                for direction, y, sign in places:
                    body(direction, y, sign, x, j)

    core = lax.rem(se, 2)
    tall_z = n_sector // 4
    z_here = lax.rem(se // 2, tall_z)
    y_here = se // (2 * tall_z)

    def at_step(dy, dz):
        return lax.rem(y_here + dy, 2) * (2 * tall_z) + lax.rem(z_here + dz, tall_z) * 2 + core

    down, up = tall_z - 1, 1
    relay_from = down + (up - down) * core
    relay_to = up + (down - up) * core

    def table_copy(k, h):
        block, target = (
            ((0, 0), (1, 0)),
            ((0, 0), (0, up)),
            ((0, 0), (0, down)),
            ((1, 0), (0, up)),
            ((1, 0), (0, down)),
            ((0, relay_from), (0, relay_to)),
            ((1, relay_from), (0, relay_to)),
        )[k]
        return pltpu.make_async_remote_copy(
            src_ref=table.at[at_step(*block), h],
            dst_ref=table.at[at_step(*block), h],
            send_sem=t_send.at[k, h],
            recv_sem=t_recv.at[k, h],
            device_id=(sl, at_step(*target)),
            device_id_type=MESH,
        )

    twin = se + 1 - 2 * core

    def twin_copy(dy, dz, h):
        return pltpu.make_async_remote_copy(
            src_ref=table.at[at_step(dy, dz), h],
            dst_ref=table.at[at_step(dy, dz), h],
            send_sem=w_send.at[dy * tall_z + dz, h],
            recv_sem=w_recv.at[dy * tall_z + dz, h],
            device_id=(sl, twin),
            device_id_type=MESH,
        )

    twins = [twin_copy(dy, dz, h) for dy in range(2) for dz in range(tall_z) for h in range(2)]

    half = n_sector // 2

    def wait_part(part):
        for j in range(nj):
            for c in load(part, j):
                c.wait()

    wait_part(0)
    wait_part(1)

    @pl.loop(0, nj)
    def _(j):
        for direction, kept, sign in ((0, 1, -0.25), (1, nx, 0.25)):
            x_out[0, direction, j] = 0.1 * field[0, kept, j, rows, :] + sign * field[3, kept, j, rows, :]

    pl.semaphore_wait(barrier, n_sector - 1 + n_slab - 1)
    x_start(W0)
    x_start(V1)
    for c in polar_copies:
        c.wait()
    for h in range(2):
        for k in range(3):
            table_copy(k, h).start()
        twin_copy(0, 0, h).start()
    wait_part(2)
    wait_part(3)

    def pack_first(direction, y, sign, x, j):
        at = pl.ds(PAD + y, 1)
        to = (x - 1, pl.ds(j, 1))
        first_out[(direction, 0) + to] = 0.1 * field[0, x, j, at, :]
        first_out[(direction, 1) + to] = 0.1 * field[1, x, j, at, :] + (0.25 * sign) * field[3, x, j, at, :]
        first_out[(direction, 2) + to] = 0.1 * field[2, x, j, at, :]

    y_rows(edges, pack_first)
    y_start(0)

    lane = lax.broadcasted_iota(I32, (8, L), 1)

    @pl.loop(1, nx + 1)
    def _(x):
        for h in range(2):

            @pl.when(x == nx // 2 - 1 + 4 * h)
            def _():
                table_copy(1, h).wait_recv()
                table_copy(2, h).wait_recv()
                table_copy(5, h).start()
                twin_copy(0, up, h).start()
                twin_copy(0, down, h).start()

            @pl.when(x == nx // 2 + 1 + 5 * h)
            def _():
                table_copy(0, h).wait_recv()
                table_copy(3, h).start()
                table_copy(4, h).start()
                twin_copy(1, 0, h).start()

        for y in range(0, ny, 8):
            here = pl.ds(PAD + y, 8)

            def sides(f, j):
                return (
                    field[f, x + 1, j, here, :],
                    field[f, x - 1, j, here, :],
                    field[f, x, j, pl.ds(PAD + y + 1, 8), :],
                    field[f, x, j, pl.ds(PAD + y - 1, 8), :],
                )

            centre = [field[3, x, j, here, :] for j in range(nj)]
            after, before = z_pair(centre, lane)
            slope = []
            for j in range(nj):
                xp, xm, yp, ym = sides(3, j)
                out_s[x - 1, pl.ds(y, 8), pl.ds(j * L, L)] = (xp + xm) + (yp + ym) + (after[j] + before[j])
                slope.append((xp - xm, yp - ym, after[j] - before[j]))
            for f in range(3):
                centre = [field[f, x, j, here, :] for j in range(nj)]
                after, before = z_pair(centre, lane)
                for j in range(nj):
                    xp, xm, yp, ym = sides(f, j)
                    total = (xp + xm) + (yp + ym) + (after[j] + before[j])
                    value = 0.4 * centre[j] + 0.1 * total - 0.25 * slope[j][f]
                    if f == 0:
                        push0[x, j, pl.ds(y, 8), :] = value
                    elif f == 1:
                        push1[x - 1, j, here, :] = value
                    else:
                        out[2, x - 1, pl.ds(y, 8), pl.ds(j * L, L)] = value

    for h in range(2):
        table_copy(5, h).wait_recv()
        twin_copy(0, 2, h).start()
        table_copy(3, h).wait_recv()
        table_copy(4, h).wait_recv()
        table_copy(6, h).start()
        twin_copy(1, up, h).start()
        twin_copy(1, down, h).start()
    x_wait_recv(W0)
    x_wait_recv(V1)
    x_start(V2)
    y_wait_recv(0)

    def add_first(direction, kept, j):
        push0[kept, j] += x_in[W0, direction, j]
        push1[kept - 1, j, rows, :] += 0.1 * x_in[V1, direction, j]

    x_faces(add_first)

    def add_first_rows(direction, y, sign, x, j):
        at = (x - 1, pl.ds(j, 1))
        push0[x, j, pl.ds(y, 1), :] += first_in[(direction, 0) + at]
        push1[x - 1, j, pl.ds(PAD + y, 1), :] += first_in[(direction, 1) + at]
        out[2, x - 1, pl.ds(y, 1), pl.ds(j * L, L)] += first_in[(direction, 2) + at]

    y_rows(far_edges, add_first_rows)

    @pl.loop(0, slots, unroll=16)
    def _(s):
        cell = cell_s[0, s]
        xy = ((cell >> 8) * 21846) >> 16
        z = cell - nz * xy
        x = xy >> 6
        y = xy & (ny - 1)
        j = z >> 7
        at = pl.ds(s, 1)
        row0[at, :] = push0[x + 1, j, pl.ds(y, 1), :]
        row1[at, :] = push1[x, j, pl.ds(y + PAD, 1), :]

    for h in range(2):
        table_copy(6, h).wait_recv()
        twin_copy(1, 2, h).start()
    for c in twins:
        c.wait_recv()

    @pl.loop(0, slots, unroll=16)
    def _(s):
        owner = owner_s[0, s]
        section = section_s[0, s]
        at = pl.ds(s, 1)
        for b in range(bins // L):
            lift_rows[b, at, :] = table[owner, 0, b, pl.ds(section, 1), :]
            drag_rows[b, at, :] = table[owner, 1, b, pl.ds(section, 1), :]
        geo0[at, :] = table[owner, 0, 0, pl.ds(sec_dev, 1), :]
        geo1[at, :] = table[owner, 1, 0, pl.ds(sec_dev, 1), :]

    diagonal = lax.broadcasted_iota(I32, (L, L), 0) == lax.broadcasted_iota(I32, (L, L), 1)
    lanes = lax.broadcasted_iota(I32, (L, L), 1).astype(F32)
    z_ids = lax.broadcasted_iota(I32, (L, nz), 1).astype(F32)
    places = lax.broadcasted_iota(I32, (L, 1), 0)
    used = count_s[0, 0]

    def column(row):
        return jnp.sum(jnp.where(diagonal, row, 0.0), axis=1, keepdims=True)

    def picked(block, lane_of):
        return jnp.sum(jnp.where(lanes == lane_of, block, 0.0), axis=1, keepdims=True)

    def xy_of(cell):
        return (((cell >> 8).astype(F32) + 0.5) * (1.0 / 3.0)).astype(I32)

    for g in range(slots // L):
        at = pl.ds(g * L, L)
        cell = cell_v[0:1, at]
        z_row = cell - nz * xy_of(cell)
        z_col = column(z_row.astype(F32))
        lane_col = column((z_row & (L - 1)).astype(F32))
        section = column(section_v[0:1, at].astype(F32))
        whole = column((owner_v[0:1, at] * sec_dev + section_v[0:1, at]).astype(F32))
        radius = 0.25 + 0.75 * (z_col + 0.5) / nz
        a = 1.0 + picked(row0[at, :], lane_col)
        t = 10.0 * radius + picked(row1[at, :], lane_col)
        chord = picked(geo0[at, :], section)
        twist = picked(geo1[at, :], section)
        position = (jnp.arctan2(a, t) - twist + 2.0) * ((bins - 1) / 4.0)
        lift, drag = 0.0, 0.0
        for b in range(bins // L):
            weight = jnp.maximum(0.0, 1.0 - jnp.abs(position - (lanes + float(b * L))))
            lift = lift + lift_rows[b, at, :] * weight
            drag = drag + drag_rows[b, at, :] * weight
        lift = jnp.sum(lift, axis=1, keepdims=True)
        drag = jnp.sum(drag, axis=1, keepdims=True)
        scale = 0.5 * chord * jnp.sqrt(a * a + t * t)
        active = places + g * L < used
        thrust = jnp.where(active, scale * (lift * t - drag * a), 0.0)
        swirl = jnp.where(active, scale * (lift * a + drag * t), 0.0)
        torque = swirl * radius
        mask = z_ids == z_col
        for c, force in ((0, 0.2 * thrust), (1, 0.2 * swirl)):
            high = force.astype(BF16).astype(F32)
            rhs[c, 0, at, :] = jnp.where(mask, high, 0.0).astype(BF16)
            rhs[c, 1, at, :] = jnp.where(mask, force - high, 0.0).astype(BF16)
        geo0[at, 0:1] = thrust
        geo1[at, 0:1] = torque
        row0[at, 0:1] = whole

    def load_copy(d):
        peer = lax.rem(se + d, n_sector)
        return pltpu.make_async_remote_copy(
            src_ref=load_send.at[peer // 2],
            dst_ref=load_recv.at[se],
            send_sem=l_send.at[d],
            recv_sem=l_recv.at[d],
            device_id=(sl, peer),
            device_id_type=MESH,
        )

    def slab_copy(d):
        return pltpu.make_async_remote_copy(
            src_ref=slab_send,
            dst_ref=slab_recv.at[sl],
            send_sem=m_send.at[d],
            recv_sem=m_recv.at[d],
            device_id=(lax.rem(sl + d, n_slab), se),
            device_id_type=MESH,
        )

    chunk = 4
    high_rows = lax.broadcasted_iota(I32, (chunk * ny, slots), 0)
    xy_all = xy_of(cell_v[...])

    def put_back(c, m):
        chosen = jnp.where(high_rows == xy_all - m * (chunk * ny), 1.0, 0.0).astype(BF16)
        total = jnp.dot(chosen, rhs[c, 0], preferred_element_type=F32) + jnp.dot(
            chosen, rhs[c, 1], preferred_element_type=F32
        )
        for k in range(chunk):
            for j in range(nj):
                piece = total[k * ny : (k + 1) * ny, j * L : (j + 1) * L]
                if c == 0:
                    push0[1 + m * chunk + k, j] += piece
                else:
                    push1[m * chunk + k, j, rows, :] += piece

    @pl.loop(0, nx // chunk)
    def _(i):
        put_back(0, jnp.where(i == 0, 0, jnp.where(i == 1, nx // chunk - 1, i - 1)))

        @pl.when(i == 1)
        def _():
            @pl.loop(0, nj)
            def _(j):
                for direction, kept, sign in ((0, 1, -0.5), (1, nx, 0.5)):
                    x_out[1, direction, j] = field[3, kept, j, rows, :] + sign * push0[kept, j]

            x_start(MID)

    @pl.loop(0, nx // chunk)
    def _(i):
        put_back(1, i)

    def pack_middle(direction, y, sign, x, j):
        at = pl.ds(PAD + y, 1)
        y_out[0, direction, x - 1, pl.ds(j, 1)] = field[3, x, j, at, :] + (0.5 * sign) * push1[x - 1, j, at, :]

    y_rows(edges, pack_middle)
    y_start(1)

    x_wait_recv(V2)

    def add_depth(direction, kept, j):
        out[2, kept - 1, :, pl.ds(j * L, L)] += 0.1 * x_in[V2, direction, j]

    x_faces(add_depth)

    @pl.loop(1, nx + 1)
    def _(x):
        for y in range(0, ny, 8):
            ys = pl.ds(y, 8)
            after, before = z_pair([out[2, x - 1, ys, pl.ds(j * L, L)] for j in range(nj)], lane)
            for j in range(nj):
                source = 0.5 * (
                    (push0[x + 1, j, ys, :] - push0[x - 1, j, ys, :])
                    + (push1[x - 1, j, pl.ds(PAD + y + 1, 8), :] - push1[x - 1, j, pl.ds(PAD + y - 1, 8), :])
                    + (after[j] - before[j])
                )
                middle = (out_s[x - 1, ys, pl.ds(j * L, L)] - source) * (1.0 / 6.0)
                field[0, x, j, pl.ds(PAD + y, 8), :] = middle
                out_s[x - 1, ys, pl.ds(j * L, L)] = source

    y_wait_recv(1)

    def add_middle_rows(direction, y, sign, x, j):
        field[0, x, j, pl.ds(PAD + y, 1), :] += (1.0 / 6.0) * y_in[0, direction, x - 1, pl.ds(j, 1)]

    y_rows(far_edges, add_middle_rows)

    def add_middle(direction, kept, j):
        field[0, kept, j, rows, :] += (1.0 / 6.0) * x_in[MID, direction, j]

    for h in halves:
        x_wait_recv(MID, (h,))
        x_faces(add_middle, h)
        for j in range(h * deep, (h + 1) * deep):
            for direction, kept, sign in ((0, 1, -0.5), (1, nx, 0.5)):
                x_out[2, direction, j] = field[0, kept, j, rows, :] + sign * push0[kept, j]
        x_start(SET, (h,))

    def pack_settled(direction, y, sign, x, j):
        at = pl.ds(PAD + y, 1)
        y_out[1, direction, x - 1, pl.ds(j, 1)] = field[0, x, j, at, :] + (0.5 * sign) * push1[x - 1, j, at, :]

    y_rows(edges, pack_settled)
    y_start(2)

    for pair in range(half):
        thrust_sum = torque_sum = 0.0
        for g in range(slots // L):
            at = pl.ds(g * L, L)
            chosen = lanes == row0[at, 0:1] - float(pair * L)
            thrust_sum = thrust_sum + jnp.where(chosen, geo0[at, 0:1], 0.0)
            torque_sum = torque_sum + jnp.where(chosen, geo1[at, 0:1], 0.0)
        load_send[pair, 0:1, :] = jnp.sum(thrust_sum, axis=0, keepdims=True)
        load_send[pair, 1:2, :] = jnp.sum(torque_sum, axis=0, keepdims=True)

    @pl.loop(1, n_sector)
    def _(d):
        load_copy(d).start()

    load_recv[se] = load_send[se // 2]

    x_wait_send(V1)

    @pl.loop(1, nx + 1)
    def _(x):
        for y in range(0, ny, 8):
            ys = pl.ds(y, 8)
            here = pl.ds(PAD + y, 8)
            after, before = z_pair([field[0, x, j, here, :] for j in range(nj)], lane)
            for j in range(nj):
                total = (
                    (field[0, x + 1, j, here, :] + field[0, x - 1, j, here, :])
                    + (field[0, x, j, pl.ds(PAD + y + 1, 8), :] + field[0, x, j, pl.ds(PAD + y - 1, 8), :])
                    + (after[j] + before[j])
                )
                settled = (total - out_s[x - 1, ys, pl.ds(j * L, L)]) * (1.0 / 6.0)
                field[1, x, j, here, :] = settled

    y_wait_recv(2)

    def add_settled_rows(direction, y, sign, x, j):
        field[1, x, j, pl.ds(PAD + y, 1), :] += (1.0 / 6.0) * y_in[1, direction, x - 1, pl.ds(j, 1)]

    y_rows(far_edges, add_settled_rows)

    def add_settled(direction, kept, j):
        field[1, kept, j, rows, :] += (1.0 / 6.0) * x_in[SET, direction, j]

    for h in halves:
        x_wait_recv(SET, (h,))
        x_faces(add_settled, h)
        x_start(COR, (h,))

    def pack_corrected(direction, y, sign, x, j):
        y_out[2, direction, x - 1, pl.ds(j, 1)] = field[1, x, j, pl.ds(PAD + y, 1), :]

    y_rows(edges, pack_corrected)
    y_start(3)

    @pl.loop(1, n_sector)
    def _(d):
        load_copy(d).wait_recv()

    mine = load_recv[0]
    for d in range(1, n_sector):
        mine = mine + load_recv[d]
    mine = jnp.where(lax.rem(se, 2) == 1, pltpu.roll(mine, L // 2, 1), mine)
    slab_send[...] = mine
    slab_recv[sl] = mine

    @pl.loop(1, n_slab)
    def _(d):
        slab_copy(d).start()

    @pl.loop(1, nx + 1)
    def _(x):
        for y in range(0, ny, 8):
            ys = pl.ds(y, 8)
            here = pl.ds(PAD + y, 8)
            centre = [field[1, x, j, here, :] for j in range(nj)]
            after, before = z_pair(centre, lane)
            for j in range(nj):
                zs = pl.ds(j * L, L)
                out_s[x - 1, ys, zs] = centre[j]
                out[0, x - 1, ys, zs] = push0[x, j, ys, :] - 0.5 * (field[1, x + 1, j, here, :] - field[1, x - 1, j, here, :])
                out[1, x - 1, ys, zs] = push1[x - 1, j, here, :] - 0.5 * (
                    field[1, x, j, pl.ds(PAD + y + 1, 8), :] - field[1, x, j, pl.ds(PAD + y - 1, 8), :]
                )
                out[2, x - 1, ys, zs] = out[2, x - 1, ys, zs] - 0.5 * (after[j] - before[j])

    y_wait_recv(3)

    def add_corrected_rows(direction, y, sign, x, j):
        out[1, x - 1, pl.ds(y, 1), pl.ds(j * L, L)] += (0.5 * sign) * y_in[2, direction, x - 1, pl.ds(j, 1)]

    y_rows(far_edges, add_corrected_rows)

    def add_corrected(direction, kept, j):
        out[0, kept - 1, :, pl.ds(j * L, L)] += (-0.5 if direction == 0 else 0.5) * x_in[COR, direction, j]

    for h in halves:
        x_wait_recv(COR, (h,))
        x_faces(add_corrected, h)

    @pl.loop(1, n_slab)
    def _(d):
        slab_copy(d).wait_recv()

    final = slab_recv[0]
    for d in range(1, n_slab):
        final = final + slab_recv[d]
    loads[...] = final[0:2, 0:sec_dev]

    for stage in (W0, V2, MID, SET, COR):
        x_wait_send(stage)
    for copies in y_all:
        for c in copies:
            c.wait_send()

    for k in range(7):
        for h in range(2):
            table_copy(k, h).wait_send()
    for c in twins:
        c.wait_send()

    @pl.loop(1, n_sector)
    def _(d):
        load_copy(d).wait_send()

    @pl.loop(1, n_slab)
    def _(d):
        slab_copy(d).wait_send()


def on_device(n_slab, n_sector, velocity, pressure, disk_cell, disk_count, disk_owner, disk_section, polar, geometry):
    nx, ny, nz = pressure.shape
    nj = nz // L
    slots = disk_cell.shape[1]
    sec_dev, bins = polar.shape[1:]
    tall = ny + 2 * PAD
    owner = disk_owner.reshape(1, slots)
    dma = pltpu.SemaphoreType.DMA
    hbm = pl.BlockSpec(memory_space=pltpu.HBM)
    vmem = pl.BlockSpec(memory_space=pltpu.VMEM)
    half = n_sector // 2
    corrected, settled, loads = pl.pallas_call(
        functools.partial(kernel, n_slab, n_sector),
        out_shape=(
            pltpu.VMEM((3, nx, ny, nz), F32),
            pltpu.VMEM((nx, ny, nz), F32),
            jax.ShapeDtypeStruct((2, sec_dev), F32),
        ),
        in_specs=[hbm] * 7 + [pl.BlockSpec(memory_space=pltpu.SMEM)],
        out_specs=(vmem, vmem, vmem),
        scratch_shapes=[
            pltpu.VMEM((4, nx + 2, nj, tall, L), F32),
            pltpu.VMEM((nx + 2, nj, ny, L), F32),
            pltpu.VMEM((nx, nj, tall, L), F32),
            pltpu.VMEM((3, 2, nj, ny, L), F32),
            pltpu.VMEM((6, 2, nj, ny, L), F32),
            pltpu.SMEM((1, slots), jnp.int32),
            pltpu.SMEM((1, slots), jnp.int32),
            pltpu.SMEM((1, slots), jnp.int32),
            pltpu.VMEM((1, slots), jnp.int32),
            pltpu.VMEM((1, slots), jnp.int32),
            pltpu.VMEM((1, slots), jnp.int32),
            pltpu.VMEM((2, sec_dev), F32),
            dma((8,)),
            pltpu.VMEM((n_sector, 2, bins // L, sec_dev + 8, L), F32),
            pltpu.VMEM((bins // L, slots, L), F32),
            pltpu.VMEM((bins // L, slots, L), F32),
            pltpu.VMEM((slots, L), F32),
            pltpu.VMEM((slots, L), F32),
            pltpu.VMEM((slots, L), F32),
            pltpu.VMEM((slots, L), F32),
            pltpu.VMEM((2, 2, slots, nz), BF16),
            pltpu.VMEM((2, 3, nx, 8, L), F32),
            pltpu.VMEM((2, 3, nx, 8, L), F32),
            pltpu.VMEM((3, 2, nx, 8, L), F32),
            pltpu.VMEM((3, 2, nx, 8, L), F32),
            pltpu.VMEM((half, 8, L), F32),
            pltpu.VMEM((n_sector, 8, L), F32),
            pltpu.VMEM((8, L), F32),
            pltpu.VMEM((n_slab, 8, L), F32),
            dma((2, 4, nj)),
            dma((bins // L,)),
            dma((6, 2, 2)),
            dma((6, 2, 2)),
            dma((4, 2)),
            dma((4, 2)),
            dma((half, 2)),
            dma((half, 2)),
            dma((half, 2)),
            dma((half, 2)),
            dma((n_sector,)),
            dma((n_sector,)),
            dma((n_slab,)),
            dma((n_slab,)),
        ],
        compiler_params=pltpu.CompilerParams(
            collective_id=0, has_side_effects=True, vmem_limit_bytes=40 * 1024 * 1024
        ),
    )(
        *(
            pltpu.with_memory_space_constraint(array, pltpu.HBM)
            for array in (velocity, pressure, disk_cell, owner, disk_section, polar, geometry)
        ),
        disk_count,
    )
    return corrected, settled, loads


def solution(mesh):
    return jax.shard_map(
        functools.partial(on_device, mesh.shape["slab"], mesh.shape["sector"]),
        mesh=mesh,
        in_specs=(
            P(None, "slab", "sector", None),
            P("slab", "sector", None),
            P("slab", "sector"),
            P("slab", "sector"),
            P("slab", "sector", None),
            P("slab", "sector"),
            P(None, "sector", None),
            P(None, "sector"),
        ),
        out_specs=(P(None, "slab", "sector", None), P("slab", "sector", None), P(None, "sector")),
        check_vma=False,
    )
```

```python
import functools

import jax
import jax.numpy as jnp
from jax import lax
from jax.experimental import pallas as pl
from jax.experimental.pallas import tpu as pltpu
from jax.sharding import PartitionSpec as P

MESH = pl.DeviceIdType.MESH
F32 = jnp.float32
I32 = jnp.int32
BF16 = jnp.bfloat16
L = 128
PAD = 8


def z_pair(tiles, lane):
    up = [pltpu.roll(t, L - 1, 1) for t in tiles]
    down = [pltpu.roll(t, 1, 1) for t in tiles]
    last = len(tiles) - 1
    zero = jnp.zeros_like(tiles[0])
    after = [jnp.where(lane == L - 1, up[j + 1] if j < last else zero, up[j]) for j in range(last + 1)]
    before = [jnp.where(lane == 0, down[j - 1] if j > 0 else zero, down[j]) for j in range(last + 1)]
    return after, before


def kernel(
    n_slab,
    n_sector,
    vel,
    pre,
    cell_h,
    owner_h,
    section_h,
    polar,
    geometry_h,
    count_s,
    out,
    out_s,
    loads,
    field,
    push0,
    push1,
    x_out,
    x_in,
    cell_s,
    owner_s,
    section_s,
    cell_v,
    owner_v,
    section_v,
    geometry,
    small_sem,
    table,
    lift_rows,
    drag_rows,
    geo0,
    geo1,
    row0,
    row1,
    rhs,
    first_out,
    first_in,
    y_out,
    y_in,
    load_send,
    load_recv,
    slab_send,
    slab_recv,
    local_sem,
    polar_sem,
    x_send,
    x_recv,
    y_send,
    y_recv,
    t_send,
    t_recv,
    w_send,
    w_recv,
    l_send,
    l_recv,
    m_send,
    m_recv,
):
    sl = lax.axis_index("slab")
    se = lax.axis_index("sector")
    nx, ny, nz = pre.shape
    nj = nz // L
    slots = cell_h.shape[1]
    sec_dev = polar.shape[1]
    bins = polar.shape[2]
    has_left = sl > 0
    has_right = sl < n_slab - 1
    rows = pl.ds(PAD, ny)

    parts = ((0, 1), (nx - 1, 1), (1, nx // 2 - 1), (nx // 2, nx // 2 - 1))

    def load(part, j):
        start, count = parts[part]
        xs = pl.ds(start, count)
        xd = pl.ds(1 + start, count)
        zs = pl.ds(j * L, L)
        return (
            pltpu.make_async_copy(vel.at[:, xs, :, zs], field.at[0:3, xd, j, rows, :], local_sem.at[0, part, j]),
            pltpu.make_async_copy(pre.at[xs, :, zs], field.at[3, xd, j, rows, :], local_sem.at[1, part, j]),
        )

    for part in range(len(parts)):
        for j in range(nj):
            for c in load(part, j):
                c.start()
    polar_copies = [
        pltpu.make_async_copy(
            polar.at[:, :, pl.ds(b * L, L)], table.at[se, :, b, pl.ds(0, sec_dev), :], polar_sem.at[b]
        )
        for b in range(bins // L)
    ]
    small_copies = [
        pltpu.make_async_copy(src, dst, small_sem.at[k])
        for k, (src, dst) in enumerate(
            (
                (geometry_h, geometry),
                (cell_h, cell_s),
                (owner_h, owner_s),
                (section_h, section_s),
                (cell_h, cell_v),
                (owner_h, owner_v),
                (section_h, section_v),
            )
        )
    ]
    for c in polar_copies + small_copies:
        c.start()

    barrier = pltpu.get_barrier_semaphore()

    @pl.loop(1, n_sector)
    def _(d):
        pl.semaphore_signal(barrier, inc=1, device_id=(sl, lax.rem(se + d, n_sector)), device_id_type=MESH)

    @pl.loop(1, n_slab)
    def _(d):
        pl.semaphore_signal(barrier, inc=1, device_id=(lax.rem(sl + d, n_slab), se), device_id_type=MESH)

    @pl.loop(1, nx + 1)
    def _(x):
        for beyond in (0, PAD + ny):
            for j in range(nj):
                for f in range(4):
                    field[f, x, j, beyond : beyond + PAD, :] = jnp.zeros((PAD, L), F32)
                push1[x - 1, j, beyond : beyond + PAD, :] = jnp.zeros((PAD, L), F32)

    for ghost in (0, nx + 1):

        @pl.loop(0, nj)
        def _(j):
            for f in range(4):
                field[f, ghost, j, rows, :] = jnp.zeros((ny, L), F32)
            push0[ghost, j] = jnp.zeros((ny, L), F32)

    for c in small_copies:
        c.wait()
    load_send[...] = jnp.zeros(load_send.shape, F32)
    for c in range(2):
        for b in range(bins // L):
            table[se, c, b, sec_dev : sec_dev + 8, :] = jnp.zeros((8, L), F32)
        table[se, c, 0, sec_dev : sec_dev + 1, 0:sec_dev] = geometry[c : c + 1, :]
    for buffer in (first_out, y_out):
        buffer[...] = jnp.zeros(buffer.shape, F32)
    W0, V1, V2, MID, SET, COR = range(6)

    halves = (0, 1)
    deep = nj // 2

    def x_copy(stage, direction, h):
        kept = 1 if direction == 0 else nx
        js = pl.ds(h * deep, deep)
        if stage in (V1, V2):
            src = field.at[stage, kept, js, rows, :]
        elif stage == COR:
            src = field.at[1, kept, js, rows, :]
        else:
            src = x_out.at[{W0: 0, MID: 1, SET: 2}[stage], direction, js]
        return pltpu.make_async_remote_copy(
            src_ref=src,
            dst_ref=x_in.at[stage, direction, js],
            send_sem=x_send.at[stage, direction, h],
            recv_sem=x_recv.at[stage, direction, h],
            device_id=(sl - 1 if direction == 0 else sl + 1, se),
            device_id_type=MESH,
        )

    def x_faces(body, h=None):
        for direction, there, kept in ((0, has_right, nx), (1, has_left, 1)):

            @pl.when(there)
            def _():
                for j in range(nj) if h is None else range(h * deep, (h + 1) * deep):
                    body(direction, kept, j)

    def x_each(act, sending, stage, parts):
        for h in parts:
            for direction, there in ((0, has_left if sending else has_right), (1, has_right if sending else has_left)):

                @pl.when(there)
                def _():
                    act(x_copy(stage, direction, h))

    def x_start(stage, parts=halves):
        x_each(lambda c: c.start(), True, stage, parts)

    def x_wait_recv(stage, parts=halves):
        x_each(lambda c: c.wait_recv(), False, stage, parts)

    def x_wait_send(stage):
        x_each(lambda c: c.wait_send(), True, stage, halves)

    below = (sl, lax.rem(se + n_sector - 1, n_sector))
    above = (sl, lax.rem(se + 1, n_sector))

    def y_copies(stage):
        return [
            pltpu.make_async_remote_copy(
                src_ref=first_out.at[direction] if stage == 0 else y_out.at[stage - 1, direction],
                dst_ref=first_in.at[direction] if stage == 0 else y_in.at[stage - 1, direction],
                send_sem=y_send.at[stage, direction],
                recv_sem=y_recv.at[stage, direction],
                device_id=(below, above)[direction],
                device_id_type=MESH,
            )
            for direction in range(2)
        ]

    y_all = [y_copies(stage) for stage in range(4)]

    def y_start(stage):
        for c in y_all[stage]:
            c.start()

    def y_wait_recv(stage):
        for c in y_all[stage]:
            c.wait_recv()

    edges = ((0, 0, -1.0), (1, ny - 1, 1.0))
    far_edges = ((0, ny - 1, -1.0), (1, 0, 1.0))

    def y_rows(places, body):
        @pl.loop(1, nx + 1)
        def _(x):
            for j in range(nj):
                for direction, y, sign in places:
                    body(direction, y, sign, x, j)

    core = lax.rem(se, 2)
    tall_z = n_sector // 4
    z_here = lax.rem(se // 2, tall_z)
    y_here = se // (2 * tall_z)

    def at_step(dy, dz):
        return lax.rem(y_here + dy, 2) * (2 * tall_z) + lax.rem(z_here + dz, tall_z) * 2 + core

    down, up = tall_z - 1, 1
    relay_from = down + (up - down) * core
    relay_to = up + (down - up) * core

    def table_copy(k, h):
        block, target = (
            ((0, 0), (1, 0)),
            ((0, 0), (0, up)),
            ((0, 0), (0, down)),
            ((1, 0), (0, up)),
            ((1, 0), (0, down)),
            ((0, relay_from), (0, relay_to)),
            ((1, relay_from), (0, relay_to)),
        )[k]
        return pltpu.make_async_remote_copy(
            src_ref=table.at[at_step(*block), h],
            dst_ref=table.at[at_step(*block), h],
            send_sem=t_send.at[k, h],
            recv_sem=t_recv.at[k, h],
            device_id=(sl, at_step(*target)),
            device_id_type=MESH,
        )

    twin = se + 1 - 2 * core

    def twin_copy(dy, dz, h):
        return pltpu.make_async_remote_copy(
            src_ref=table.at[at_step(dy, dz), h],
            dst_ref=table.at[at_step(dy, dz), h],
            send_sem=w_send.at[dy * tall_z + dz, h],
            recv_sem=w_recv.at[dy * tall_z + dz, h],
            device_id=(sl, twin),
            device_id_type=MESH,
        )

    twins = [twin_copy(dy, dz, h) for dy in range(2) for dz in range(tall_z) for h in range(2)]

    half = n_sector // 2

    def wait_part(part):
        for j in range(nj):
            for c in load(part, j):
                c.wait()

    wait_part(0)
    wait_part(1)

    @pl.loop(0, nj)
    def _(j):
        for direction, kept, sign in ((0, 1, -0.25), (1, nx, 0.25)):
            x_out[0, direction, j] = 0.1 * field[0, kept, j, rows, :] + sign * field[3, kept, j, rows, :]

    pl.semaphore_wait(barrier, n_sector - 1 + n_slab - 1)
    x_start(W0)
    x_start(V1)
    for c in polar_copies:
        c.wait()
    for h in range(2):
        for k in range(3):
            table_copy(k, h).start()
        twin_copy(0, 0, h).start()
    wait_part(2)
    wait_part(3)

    def pack_first(direction, y, sign, x, j):
        at = pl.ds(PAD + y, 1)
        to = (x - 1, pl.ds(j, 1))
        first_out[(direction, 0) + to] = 0.1 * field[0, x, j, at, :]
        first_out[(direction, 1) + to] = 0.1 * field[1, x, j, at, :] + (0.25 * sign) * field[3, x, j, at, :]
        first_out[(direction, 2) + to] = 0.1 * field[2, x, j, at, :]

    y_rows(edges, pack_first)
    y_start(0)

    lane = lax.broadcasted_iota(I32, (8, L), 1)

    @pl.loop(1, nx + 1)
    def _(x):
        for h in range(2):

            @pl.when(x == nx // 2 - 1 + 4 * h)
            def _():
                table_copy(1, h).wait_recv()
                table_copy(2, h).wait_recv()
                table_copy(5, h).start()
                twin_copy(0, up, h).start()
                twin_copy(0, down, h).start()

            @pl.when(x == nx // 2 + 1 + 5 * h)
            def _():
                table_copy(0, h).wait_recv()
                table_copy(3, h).start()
                table_copy(4, h).start()
                twin_copy(1, 0, h).start()

        for y in range(0, ny, 8):
            here = pl.ds(PAD + y, 8)

            def sides(f, j):
                return (
                    field[f, x + 1, j, here, :],
                    field[f, x - 1, j, here, :],
                    field[f, x, j, pl.ds(PAD + y + 1, 8), :],
                    field[f, x, j, pl.ds(PAD + y - 1, 8), :],
                )

            centre = [field[3, x, j, here, :] for j in range(nj)]
            after, before = z_pair(centre, lane)
            slope = []
            for j in range(nj):
                xp, xm, yp, ym = sides(3, j)
                out_s[x - 1, pl.ds(y, 8), pl.ds(j * L, L)] = (xp + xm) + (yp + ym) + (after[j] + before[j])
                slope.append((xp - xm, yp - ym, after[j] - before[j]))
            for f in range(3):
                centre = [field[f, x, j, here, :] for j in range(nj)]
                after, before = z_pair(centre, lane)
                for j in range(nj):
                    xp, xm, yp, ym = sides(f, j)
                    total = (xp + xm) + (yp + ym) + (after[j] + before[j])
                    value = 0.4 * centre[j] + 0.1 * total - 0.25 * slope[j][f]
                    if f == 0:
                        push0[x, j, pl.ds(y, 8), :] = value
                    elif f == 1:
                        push1[x - 1, j, here, :] = value
                    else:
                        out[2, x - 1, pl.ds(y, 8), pl.ds(j * L, L)] = value

    for h in range(2):
        table_copy(5, h).wait_recv()
        twin_copy(0, 2, h).start()
        table_copy(3, h).wait_recv()
        table_copy(4, h).wait_recv()
        table_copy(6, h).start()
        twin_copy(1, up, h).start()
        twin_copy(1, down, h).start()
    x_wait_recv(W0)
    x_wait_recv(V1)
    x_start(V2)
    y_wait_recv(0)

    def add_first(direction, kept, j):
        push0[kept, j] += x_in[W0, direction, j]
        push1[kept - 1, j, rows, :] += 0.1 * x_in[V1, direction, j]

    x_faces(add_first)

    def add_first_rows(direction, y, sign, x, j):
        at = (x - 1, pl.ds(j, 1))
        push0[x, j, pl.ds(y, 1), :] += first_in[(direction, 0) + at]
        push1[x - 1, j, pl.ds(PAD + y, 1), :] += first_in[(direction, 1) + at]
        out[2, x - 1, pl.ds(y, 1), pl.ds(j * L, L)] += first_in[(direction, 2) + at]

    y_rows(far_edges, add_first_rows)

    @pl.loop(0, slots, unroll=16)
    def _(s):
        cell = cell_s[0, s]
        xy = ((cell >> 8) * 21846) >> 16
        z = cell - nz * xy
        x = xy >> 6
        y = xy & (ny - 1)
        j = z >> 7
        at = pl.ds(s, 1)
        row0[at, :] = push0[x + 1, j, pl.ds(y, 1), :]
        row1[at, :] = push1[x, j, pl.ds(y + PAD, 1), :]

    diagonal = lax.broadcasted_iota(I32, (L, L), 0) == lax.broadcasted_iota(I32, (L, L), 1)
    lanes = lax.broadcasted_iota(I32, (L, L), 1).astype(F32)
    z_ids = lax.broadcasted_iota(I32, (L, nz), 1).astype(F32)
    places = lax.broadcasted_iota(I32, (L, 1), 0)
    used = count_s[0, 0]

    def column(row):
        return jnp.sum(jnp.where(diagonal, row, 0.0), axis=1, keepdims=True)

    def picked(block, lane_of):
        return jnp.sum(jnp.where(lanes == lane_of, block, 0.0), axis=1, keepdims=True)

    def xy_of(cell):
        return (((cell >> 8).astype(F32) + 0.5) * (1.0 / 3.0)).astype(I32)

    flow = []
    for g in range(slots // L):
        at = pl.ds(g * L, L)
        cell = cell_v[0:1, at]
        z_row = cell - nz * xy_of(cell)
        z_col = column(z_row.astype(F32))
        lane_col = column((z_row & (L - 1)).astype(F32))
        section = column(section_v[0:1, at].astype(F32))
        whole = column((owner_v[0:1, at] * sec_dev + section_v[0:1, at]).astype(F32))
        radius = 0.25 + 0.75 * (z_col + 0.5) / nz
        a = 1.0 + picked(row0[at, :], lane_col)
        t = 10.0 * radius + picked(row1[at, :], lane_col)
        speed = jnp.where(places + g * L < used, 0.5 * jnp.sqrt(a * a + t * t), 0.0)
        row0[at, 0:1] = whole
        flow.append((z_col, section, radius, a, t, jnp.arctan2(a, t), speed))

    for h in range(2):
        table_copy(6, h).wait_recv()
        twin_copy(1, 2, h).start()
    for c in twins:
        c.wait_recv()

    @pl.loop(0, slots, unroll=16)
    def _(s):
        owner = owner_s[0, s]
        section = section_s[0, s]
        at = pl.ds(s, 1)
        for b in range(bins // L):
            lift_rows[b, at, :] = table[owner, 0, b, pl.ds(section, 1), :]
            drag_rows[b, at, :] = table[owner, 1, b, pl.ds(section, 1), :]
        geo0[at, :] = table[owner, 0, 0, pl.ds(sec_dev, 1), :]
        geo1[at, :] = table[owner, 1, 0, pl.ds(sec_dev, 1), :]

    for g in range(slots // L):
        at = pl.ds(g * L, L)
        z_col, section, radius, a, t, angle, speed = flow[g]
        chord = picked(geo0[at, :], section)
        twist = picked(geo1[at, :], section)
        position = (angle - twist + 2.0) * ((bins - 1) / 4.0)
        lift, drag = 0.0, 0.0
        for b in range(bins // L):
            weight = jnp.maximum(0.0, 1.0 - jnp.abs(position - (lanes + float(b * L))))
            lift = lift + lift_rows[b, at, :] * weight
            drag = drag + drag_rows[b, at, :] * weight
        lift = jnp.sum(lift, axis=1, keepdims=True)
        drag = jnp.sum(drag, axis=1, keepdims=True)
        scale = speed * chord
        thrust = scale * (lift * t - drag * a)
        swirl = scale * (lift * a + drag * t)
        mask = z_ids == z_col
        for c, force in ((0, 0.2 * thrust), (1, 0.2 * swirl)):
            high = force.astype(BF16).astype(F32)
            rhs[c, 0, at, :] = jnp.where(mask, high, 0.0).astype(BF16)
            rhs[c, 1, at, :] = jnp.where(mask, force - high, 0.0).astype(BF16)
        geo0[at, 0:1] = thrust
        geo1[at, 0:1] = swirl * radius

    def load_copy(d):
        peer = lax.rem(se + d, n_sector)
        return pltpu.make_async_remote_copy(
            src_ref=load_send.at[peer // 2],
            dst_ref=load_recv.at[se],
            send_sem=l_send.at[d],
            recv_sem=l_recv.at[d],
            device_id=(sl, peer),
            device_id_type=MESH,
        )

    def slab_copy(d):
        return pltpu.make_async_remote_copy(
            src_ref=slab_send,
            dst_ref=slab_recv.at[sl],
            send_sem=m_send.at[d],
            recv_sem=m_recv.at[d],
            device_id=(lax.rem(sl + d, n_slab), se),
            device_id_type=MESH,
        )

    chunk = 4
    high_rows = lax.broadcasted_iota(I32, (chunk * ny, slots), 0)
    xy_all = xy_of(cell_v[...])

    def put_back(c, m):
        chosen = jnp.where(high_rows == xy_all - m * (chunk * ny), 1.0, 0.0).astype(BF16)
        total = jnp.dot(chosen, rhs[c, 0], preferred_element_type=F32) + jnp.dot(
            chosen, rhs[c, 1], preferred_element_type=F32
        )
        for k in range(chunk):
            for j in range(nj):
                piece = total[k * ny : (k + 1) * ny, j * L : (j + 1) * L]
                if c == 0:
                    push0[1 + m * chunk + k, j] += piece
                else:
                    push1[m * chunk + k, j, rows, :] += piece

    @pl.loop(0, nx // chunk)
    def _(i):
        put_back(0, jnp.where(i == 0, 0, jnp.where(i == 1, nx // chunk - 1, i - 1)))

        @pl.when(i == 1)
        def _():
            @pl.loop(0, nj)
            def _(j):
                for direction, kept, sign in ((0, 1, -0.5), (1, nx, 0.5)):
                    x_out[1, direction, j] = field[3, kept, j, rows, :] + sign * push0[kept, j]

            x_start(MID)

    @pl.loop(0, nx // chunk)
    def _(i):
        put_back(1, i)

    def pack_middle(direction, y, sign, x, j):
        at = pl.ds(PAD + y, 1)
        y_out[0, direction, x - 1, pl.ds(j, 1)] = field[3, x, j, at, :] + (0.5 * sign) * push1[x - 1, j, at, :]

    y_rows(edges, pack_middle)
    y_start(1)

    x_wait_recv(V2)

    def add_depth(direction, kept, j):
        out[2, kept - 1, :, pl.ds(j * L, L)] += 0.1 * x_in[V2, direction, j]

    x_faces(add_depth)

    @pl.loop(1, nx + 1)
    def _(x):
        for y in range(0, ny, 8):
            ys = pl.ds(y, 8)
            after, before = z_pair([out[2, x - 1, ys, pl.ds(j * L, L)] for j in range(nj)], lane)
            for j in range(nj):
                source = 0.5 * (
                    (push0[x + 1, j, ys, :] - push0[x - 1, j, ys, :])
                    + (push1[x - 1, j, pl.ds(PAD + y + 1, 8), :] - push1[x - 1, j, pl.ds(PAD + y - 1, 8), :])
                    + (after[j] - before[j])
                )
                middle = (out_s[x - 1, ys, pl.ds(j * L, L)] - source) * (1.0 / 6.0)
                field[0, x, j, pl.ds(PAD + y, 8), :] = middle
                out_s[x - 1, ys, pl.ds(j * L, L)] = source

    y_wait_recv(1)

    def add_middle_rows(direction, y, sign, x, j):
        field[0, x, j, pl.ds(PAD + y, 1), :] += (1.0 / 6.0) * y_in[0, direction, x - 1, pl.ds(j, 1)]

    y_rows(far_edges, add_middle_rows)

    def add_middle(direction, kept, j):
        field[0, kept, j, rows, :] += (1.0 / 6.0) * x_in[MID, direction, j]

    for h in halves:
        x_wait_recv(MID, (h,))
        x_faces(add_middle, h)
        for j in range(h * deep, (h + 1) * deep):
            for direction, kept, sign in ((0, 1, -0.5), (1, nx, 0.5)):
                x_out[2, direction, j] = field[0, kept, j, rows, :] + sign * push0[kept, j]
        x_start(SET, (h,))

    def pack_settled(direction, y, sign, x, j):
        at = pl.ds(PAD + y, 1)
        y_out[1, direction, x - 1, pl.ds(j, 1)] = field[0, x, j, at, :] + (0.5 * sign) * push1[x - 1, j, at, :]

    y_rows(edges, pack_settled)
    y_start(2)

    for pair in range(half):
        thrust_sum = torque_sum = 0.0
        for g in range(slots // L):
            at = pl.ds(g * L, L)
            chosen = lanes == row0[at, 0:1] - float(pair * L)
            thrust_sum = thrust_sum + jnp.where(chosen, geo0[at, 0:1], 0.0)
            torque_sum = torque_sum + jnp.where(chosen, geo1[at, 0:1], 0.0)
        load_send[pair, 0:1, :] = jnp.sum(thrust_sum, axis=0, keepdims=True)
        load_send[pair, 1:2, :] = jnp.sum(torque_sum, axis=0, keepdims=True)

    @pl.loop(1, n_sector)
    def _(d):
        load_copy(d).start()

    load_recv[se] = load_send[se // 2]

    x_wait_send(V1)

    @pl.loop(1, nx + 1)
    def _(x):
        for y in range(0, ny, 8):
            ys = pl.ds(y, 8)
            here = pl.ds(PAD + y, 8)
            after, before = z_pair([field[0, x, j, here, :] for j in range(nj)], lane)
            for j in range(nj):
                total = (
                    (field[0, x + 1, j, here, :] + field[0, x - 1, j, here, :])
                    + (field[0, x, j, pl.ds(PAD + y + 1, 8), :] + field[0, x, j, pl.ds(PAD + y - 1, 8), :])
                    + (after[j] + before[j])
                )
                settled = (total - out_s[x - 1, ys, pl.ds(j * L, L)]) * (1.0 / 6.0)
                field[1, x, j, here, :] = settled

    y_wait_recv(2)

    def add_settled_rows(direction, y, sign, x, j):
        field[1, x, j, pl.ds(PAD + y, 1), :] += (1.0 / 6.0) * y_in[1, direction, x - 1, pl.ds(j, 1)]

    y_rows(far_edges, add_settled_rows)

    def add_settled(direction, kept, j):
        field[1, kept, j, rows, :] += (1.0 / 6.0) * x_in[SET, direction, j]

    for h in halves:
        x_wait_recv(SET, (h,))
        x_faces(add_settled, h)
        x_start(COR, (h,))

    def pack_corrected(direction, y, sign, x, j):
        y_out[2, direction, x - 1, pl.ds(j, 1)] = field[1, x, j, pl.ds(PAD + y, 1), :]

    y_rows(edges, pack_corrected)
    y_start(3)

    @pl.loop(1, n_sector)
    def _(d):
        load_copy(d).wait_recv()

    mine = load_recv[0]
    for d in range(1, n_sector):
        mine = mine + load_recv[d]
    mine = jnp.where(lax.rem(se, 2) == 1, pltpu.roll(mine, L // 2, 1), mine)
    slab_send[...] = mine
    slab_recv[sl] = mine

    @pl.loop(1, n_slab)
    def _(d):
        slab_copy(d).start()

    @pl.loop(1, nx + 1)
    def _(x):
        for y in range(0, ny, 8):
            ys = pl.ds(y, 8)
            here = pl.ds(PAD + y, 8)
            centre = [field[1, x, j, here, :] for j in range(nj)]
            after, before = z_pair(centre, lane)
            for j in range(nj):
                zs = pl.ds(j * L, L)
                out_s[x - 1, ys, zs] = centre[j]
                out[0, x - 1, ys, zs] = push0[x, j, ys, :] - 0.5 * (field[1, x + 1, j, here, :] - field[1, x - 1, j, here, :])
                out[1, x - 1, ys, zs] = push1[x - 1, j, here, :] - 0.5 * (
                    field[1, x, j, pl.ds(PAD + y + 1, 8), :] - field[1, x, j, pl.ds(PAD + y - 1, 8), :]
                )
                out[2, x - 1, ys, zs] = out[2, x - 1, ys, zs] - 0.5 * (after[j] - before[j])

    y_wait_recv(3)

    def add_corrected_rows(direction, y, sign, x, j):
        out[1, x - 1, pl.ds(y, 1), pl.ds(j * L, L)] += (0.5 * sign) * y_in[2, direction, x - 1, pl.ds(j, 1)]

    y_rows(far_edges, add_corrected_rows)

    def add_corrected(direction, kept, j):
        out[0, kept - 1, :, pl.ds(j * L, L)] += (-0.5 if direction == 0 else 0.5) * x_in[COR, direction, j]

    for h in halves:
        x_wait_recv(COR, (h,))
        x_faces(add_corrected, h)

    @pl.loop(1, n_slab)
    def _(d):
        slab_copy(d).wait_recv()

    final = slab_recv[0]
    for d in range(1, n_slab):
        final = final + slab_recv[d]
    loads[...] = final[0:2, 0:sec_dev]

    for stage in (W0, V2, MID, SET, COR):
        x_wait_send(stage)
    for copies in y_all:
        for c in copies:
            c.wait_send()

    for k in range(7):
        for h in range(2):
            table_copy(k, h).wait_send()
    for c in twins:
        c.wait_send()

    @pl.loop(1, n_sector)
    def _(d):
        load_copy(d).wait_send()

    @pl.loop(1, n_slab)
    def _(d):
        slab_copy(d).wait_send()


def write_back(fields, settled, loads, fields_out, settled_out, loads_out, sems):
    pairs = [(fields.at[k], fields_out.at[k]) for k in range(3)] + [(settled, settled_out), (loads, loads_out)]
    copies = [pltpu.make_async_copy(src, dst, sems.at[k]) for k, (src, dst) in enumerate(pairs)]
    for c in copies:
        c.start()
    for c in copies:
        c.wait()


def on_device(n_slab, n_sector, velocity, pressure, disk_cell, disk_count, disk_owner, disk_section, polar, geometry):
    nx, ny, nz = pressure.shape
    nj = nz // L
    slots = disk_cell.shape[1]
    sec_dev, bins = polar.shape[1:]
    tall = ny + 2 * PAD
    owner = disk_owner.reshape(1, slots)
    dma = pltpu.SemaphoreType.DMA
    hbm = pl.BlockSpec(memory_space=pltpu.HBM)
    vmem = pl.BlockSpec(memory_space=pltpu.VMEM)
    half = n_sector // 2
    corrected, settled, loads = pl.pallas_call(
        functools.partial(kernel, n_slab, n_sector),
        out_shape=(
            pltpu.VMEM((3, nx, ny, nz), F32),
            pltpu.VMEM((nx, ny, nz), F32),
            pltpu.VMEM((2, sec_dev), F32),
        ),
        in_specs=[hbm] * 7 + [pl.BlockSpec(memory_space=pltpu.SMEM)],
        out_specs=(vmem, vmem, vmem),
        scratch_shapes=[
            pltpu.VMEM((4, nx + 2, nj, tall, L), F32),
            pltpu.VMEM((nx + 2, nj, ny, L), F32),
            pltpu.VMEM((nx, nj, tall, L), F32),
            pltpu.VMEM((3, 2, nj, ny, L), F32),
            pltpu.VMEM((6, 2, nj, ny, L), F32),
            pltpu.SMEM((1, slots), jnp.int32),
            pltpu.SMEM((1, slots), jnp.int32),
            pltpu.SMEM((1, slots), jnp.int32),
            pltpu.VMEM((1, slots), jnp.int32),
            pltpu.VMEM((1, slots), jnp.int32),
            pltpu.VMEM((1, slots), jnp.int32),
            pltpu.VMEM((2, sec_dev), F32),
            dma((8,)),
            pltpu.VMEM((n_sector, 2, bins // L, sec_dev + 8, L), F32),
            pltpu.VMEM((bins // L, slots, L), F32),
            pltpu.VMEM((bins // L, slots, L), F32),
            pltpu.VMEM((slots, L), F32),
            pltpu.VMEM((slots, L), F32),
            pltpu.VMEM((slots, L), F32),
            pltpu.VMEM((slots, L), F32),
            pltpu.VMEM((2, 2, slots, nz), BF16),
            pltpu.VMEM((2, 3, nx, 8, L), F32),
            pltpu.VMEM((2, 3, nx, 8, L), F32),
            pltpu.VMEM((3, 2, nx, 8, L), F32),
            pltpu.VMEM((3, 2, nx, 8, L), F32),
            pltpu.VMEM((half, 8, L), F32),
            pltpu.VMEM((n_sector, 8, L), F32),
            pltpu.VMEM((8, L), F32),
            pltpu.VMEM((n_slab, 8, L), F32),
            dma((2, 4, nj)),
            dma((bins // L,)),
            dma((6, 2, 2)),
            dma((6, 2, 2)),
            dma((4, 2)),
            dma((4, 2)),
            dma((half, 2)),
            dma((half, 2)),
            dma((half, 2)),
            dma((half, 2)),
            dma((n_sector,)),
            dma((n_sector,)),
            dma((n_slab,)),
            dma((n_slab,)),
        ],
        compiler_params=pltpu.CompilerParams(
            collective_id=0, has_side_effects=True, vmem_limit_bytes=40 * 1024 * 1024
        ),
    )(
        *(
            pltpu.with_memory_space_constraint(array, pltpu.HBM)
            for array in (velocity, pressure, disk_cell, owner, disk_section, polar, geometry)
        ),
        disk_count,
    )
    return pl.pallas_call(
        write_back,
        out_shape=(
            jax.ShapeDtypeStruct((3, nx, ny, nz), F32),
            jax.ShapeDtypeStruct((nx, ny, nz), F32),
            jax.ShapeDtypeStruct((2, sec_dev), F32),
        ),
        in_specs=[vmem] * 3,
        out_specs=(hbm,) * 3,
        scratch_shapes=[dma((5,))],
        compiler_params=pltpu.CompilerParams(vmem_limit_bytes=1024 * 1024),
    )(*(pltpu.with_memory_space_constraint(array, pltpu.VMEM) for array in (corrected, settled, loads)))


def solution(mesh):
    return jax.shard_map(
        functools.partial(on_device, mesh.shape["slab"], mesh.shape["sector"]),
        mesh=mesh,
        in_specs=(
            P(None, "slab", "sector", None),
            P("slab", "sector", None),
            P("slab", "sector"),
            P("slab", "sector"),
            P("slab", "sector", None),
            P("slab", "sector"),
            P(None, "sector", None),
            P(None, "sector"),
        ),
        out_specs=(P(None, "slab", "sector", None), P("slab", "sector", None), P(None, "sector")),
        check_vma=False,
    )
```
